256 devices in a mesh: gx: 16 (over y, z_lo, core), gy: 4 (over z_hi), gz: 4 (over x).
Axes of the slice: x: 4, y: 4, z: 8 (z_hi: 4, z_lo: 2; z = z_hi * 2 + z_lo), core: 2. Of those that a mesh axis runs over, the one named last changes fastest.
Arguments:
- positions: float32 [3, 65536], P(None, ('gx', 'gy', 'gz')), may hold values from 0 to 1
- species: int32 [65536], P(('gx', 'gy', 'gz')), may hold values from 0 to 3
- neighbors: int32 [64, 65536], P(None, ('gx', 'gy', 'gz')), may hold values from 0 to 768, as said below
- atom_count: int32 [256], P(('gx', 'gy', 'gz')), may hold values from 32 to 256, as said below
- ghost_x: int32 [256, 2, 128], P(('gx', 'gy', 'gz')), may hold values from 0 to 255, as said below
- ghost_yz: int32 [256, 4, 64], P(('gx', 'gy', 'gz')), may hold values from 0 to 255, as said below
- embedding: bfloat16 [4, 512], replicated, may hold values from -6 to 6
- filters: bfloat16 [2, 8, 512], replicated, may hold values from -2 to 2
- update_u: bfloat16 [2, 4, 128, 128], replicated, may hold values from -0.5 to 0.5
- update_v: bfloat16 [2, 4, 128, 128], replicated, may hold values from -0.5 to 0.5
- force_w: bfloat16 [4, 128, 8], replicated, may hold values from -0.5 to 0.5
Outputs:
- force_mean: float32 [3, 65536], P(None, ('gx', 'gy', 'gz'))
- deviation: float32 [65536], P(('gx', 'gy', 'gz'))
The draws below stay inside these ranges and needn't reach their ends.
Inputs may be any that keep to these rules, and one draw needn't show every extreme that they name: `atom_count`: each domain holds 256 // 2**k live atoms for some k of 0 to 3; at least one domain holds exactly 256. `ghost_x`: indices of live atoms of the lending domain (below its atom_count); entry 0 of face 0 is its last live atom. `ghost_yz`: indices of live atoms of the lending domain (below its atom_count). `neighbors`: for a live atom, slots 0 to 31 hold a live own atom or the empty mark 256 + 8 * 64; the other slots hold the empty mark or a ghost row of a face that the atom lies near: ten times its coordinate along that face's axis is below 2 for a lower face, 8 or more for an upper one. A dead atom's slots are all empty. Slot 0 of each domain's first atom is 0.
All inputs are finite; a program needn't handle non-finite values.
Results may differ from the reference program's by a relative error of at most 0.02.
Values sent between devices are 32-bit elements; how exact they have to be, the bound alone decides.
A program may use at most 64 MiB of HBM per device.

```python
import jax
import jax.numpy as jnp
from jax import lax

ATOMS_DEV = 256
GHOST = 64
MODELS = 4
C = 128
KB = 8
SPECIES = 4
LAYERS = 2
NBR_LOCAL = 32
NBR_GHOST = 32
NBR = 64
ATOMS = 65536
N_GX = 16
N_GY = 4
N_GZ = 4


def live_counts(key):
    seeded = jax.random.fold_in(key, 101)
    devices_n = ATOMS // ATOMS_DEV
    levels = jax.random.randint(jax.random.fold_in(seeded, 1), (devices_n,), 0, 4)
    counts = ATOMS_DEV // jnp.power(2, levels)
    heavy = jax.random.randint(jax.random.fold_in(seeded, 2), (), 0, devices_n)
    return jnp.where(jnp.arange(devices_n) == heavy, ATOMS_DEV, counts).astype(jnp.int32)


def cell_grid(key):
    return jax.random.randint(jax.random.fold_in(key, 505), (3, ATOMS), 0, 10)


def draw_positions(key, part):
    cells = cell_grid(key).astype(jnp.float32)
    inside = jax.random.uniform(jax.random.fold_in(key, 506), (3, ATOMS), jnp.float32)
    return (0.1 * (cells + inside)).astype(jnp.float32)


def draw_atom_count(key, part):
    return live_counts(key)


def draw_ghost_x(key, part):
    counts = live_counts(key)
    devices_n = ATOMS // ATOMS_DEV
    chosen = jax.random.randint(jax.random.fold_in(key, 202), (devices_n, 2, 2 * GHOST), 0, counts[:, None, None])
    return chosen.at[:, 0, 0].set(counts - 1).astype(jnp.int32)


def draw_ghost_yz(key, part):
    counts = live_counts(key)
    devices_n = ATOMS // ATOMS_DEV
    chosen = jax.random.randint(jax.random.fold_in(key, 303), (devices_n, 4, GHOST), 0, counts[:, None, None])
    return chosen.astype(jnp.int32)


def draw_neighbors(key, part):
    counts = live_counts(key)
    devices_n = ATOMS // ATOMS_DEV
    empty_mark = ATOMS_DEV + 8 * GHOST
    cells = cell_grid(key).reshape(3, devices_n, ATOMS_DEV)
    near_faces = jnp.stack([cells[0] < 2, cells[0] >= 8, cells[1] < 2, cells[1] >= 8, cells[2] < 2, cells[2] >= 8], axis=0)
    any_near = jnp.any(near_faces, axis=0)
    alive_rows = jnp.arange(ATOMS_DEV)[None, :] < counts[:, None]
    local_ids = jax.random.randint(jax.random.fold_in(key, 404), (NBR_LOCAL, devices_n, ATOMS_DEV), 0, counts[None, :, None])
    local_gap = jax.random.randint(jax.random.fold_in(key, 405), (NBR_LOCAL, devices_n, ATOMS_DEV), 0, 5) == 0
    local_ids = jnp.where(local_gap | jnp.logical_not(alive_rows)[None], empty_mark, local_ids)
    scores = jax.random.randint(jax.random.fold_in(key, 408), (NBR_GHOST, 6, devices_n, ATOMS_DEV), 0, 1024) * 8
    scores = scores + jnp.arange(6)[None, :, None, None] + 16384 * near_faces.astype(jnp.int32)[None]
    face = jnp.argmax(scores, axis=1).astype(jnp.int32)
    starts = jnp.array([0, 2 * GHOST, 4 * GHOST, 5 * GHOST, 6 * GHOST, 7 * GHOST], jnp.int32)
    widths = jnp.array([2 * GHOST, 2 * GHOST, GHOST, GHOST, GHOST, GHOST], jnp.int32)
    offset = jax.random.randint(jax.random.fold_in(key, 406), (NBR_GHOST, devices_n, ATOMS_DEV), 0, widths[face])
    ghost_ids = ATOMS_DEV + starts[face] + offset
    ghost_gap = jax.random.randint(jax.random.fold_in(key, 407), (NBR_GHOST, devices_n, ATOMS_DEV), 0, 4) == 0
    drop = ghost_gap | jnp.logical_not(alive_rows)[None] | jnp.logical_not(any_near)[None]
    ghost_ids = jnp.where(drop, empty_mark, ghost_ids)
    joined = jnp.concatenate([local_ids, ghost_ids], axis=0)
    joined = joined.at[0, :, 0].set(0)
    return joined.reshape(NBR, ATOMS).astype(jnp.int32)


def plant(values, stream_key, low, top_value):
    place = [jax.random.randint(jax.random.fold_in(stream_key, axis), (), 0, length) for axis, length in enumerate(values.shape)]
    longest = values.shape.index(max(values.shape))
    neighbour = place[:longest] + [(place[longest] + 1) % values.shape[longest]] + place[longest + 1:]
    return values.at[tuple(place)].set(low).at[tuple(neighbour)].set(top_value)


def bell_draw(rng, dims, scale, most, kind=jnp.bfloat16):
    values = jax.random.normal(rng, dims, jnp.float32) * scale
    return jnp.minimum(jnp.maximum(values, -most), most).astype(kind)


def setup_inputs(seed: int = 0) -> dict:
    key_of = jax.random.split(jax.random.key(seed), 12)
    positions = draw_positions(jax.random.fold_in(key_of[11], 71), 0)
    species = plant(jax.random.randint(key_of[1], (ATOMS,), 0, SPECIES), jax.random.fold_in(key_of[1], 1), 0, SPECIES - 1).astype(jnp.int32)
    neighbors = draw_neighbors(jax.random.fold_in(key_of[11], 71), 0)
    atom_count = draw_atom_count(jax.random.fold_in(key_of[11], 71), 0)
    ghost_x = draw_ghost_x(jax.random.fold_in(key_of[11], 71), 0)
    ghost_yz = draw_ghost_yz(jax.random.fold_in(key_of[11], 71), 0)
    embedding = bell_draw(key_of[6], (SPECIES, MODELS * C), 1.0, 6.0)
    filters = bell_draw(key_of[7], (LAYERS, KB, MODELS * C), KB ** -0.5, 2.0)
    update_u = bell_draw(key_of[8], (LAYERS, MODELS, C, C), C ** -0.5, 0.5)
    update_v = bell_draw(key_of[9], (LAYERS, MODELS, C, C), C ** -0.5, 0.5)
    force_w = bell_draw(key_of[10], (MODELS, C, KB), C ** -0.5, 0.5)
    return {"positions": positions, "species": species, "neighbors": neighbors, "atom_count": atom_count, "ghost_x": ghost_x, "ghost_yz": ghost_yz, "embedding": embedding, "filters": filters, "update_u": update_u, "update_v": update_v, "force_w": force_w}


EDGE_LENGTH_SCALE = 0.125
SPACING = 0.5
SHARPNESS = 2.0


def radial(squared, count_basis):
    centres = SPACING * jnp.arange(count_basis, dtype=jnp.float32)
    return jnp.exp(-jnp.square((squared[None] - centres.reshape((count_basis,) + (1,) * squared.ndim)) * SHARPNESS))


def ghosts_of(source, x_lists, yz_lists, shift_pos):
    face_list = [(x_lists, 0, 0, 1), (x_lists, 1, 0, -1), (yz_lists, 0, 1, 1), (yz_lists, 1, 1, -1), (yz_lists, 2, 2, 1), (yz_lists, 3, 2, -1)]
    pieces = []
    for chooser, face_no, axis_no, offset in face_list:
        chosen = jnp.take_along_axis(source, chooser[:, :, :, face_no, :, None], axis=3)
        rolled = jnp.roll(chosen, offset, axis=axis_no)
        if shift_pos:
            rolled = rolled - offset * (jnp.arange(source.shape[4]) == axis_no).astype(jnp.float32)
        pieces.append(rolled)
    return jnp.concatenate(pieces, axis=3)


def geometry(pos_tab, slot_ids):
    empty_row = pos_tab.shape[0] - 1
    centre = pos_tab[:ATOMS_DEV]
    present = (slot_ids < empty_row).astype(jnp.float32)
    displacement_vectors = pos_tab[slot_ids] - centre[None]
    radial_terms = radial(jnp.sum(displacement_vectors * displacement_vectors, axis=2), KB) * present[None]
    return displacement_vectors, radial_terms


def rounded(values):
    return lax.optimization_barrier(values.astype(jnp.bfloat16)).astype(jnp.float32).reshape(ATOMS_DEV, MODELS, C)


def layer_dev(member, filter_w, mat_u, mat_v):
    pos_tab, feat_tab, slot_ids = member
    displacement_vectors, radial_terms = geometry(pos_tab, slot_ids)
    weights = jnp.einsum("ksa,kc->sac", radial_terms, filter_w)
    summed_messages = EDGE_LENGTH_SCALE * jnp.sum(weights * feat_tab[slot_ids], axis=0)
    current = feat_tab[:ATOMS_DEV]
    pre_act = jnp.einsum("amc,mce->ame", rounded(summed_messages), mat_u) + jnp.einsum("amc,mce->ame", rounded(current), mat_v)
    return current + jax.nn.silu(pre_act).reshape(ATOMS_DEV, MODELS * C)


def reference(positions, species, neighbors, atom_count, ghost_x, ghost_yz, embedding, filters, update_u, update_v, force_w):
    devices_n = N_GX * N_GY * N_GZ
    grid_shape = (N_GX, N_GY, N_GZ, ATOMS_DEV)
    x_lists = ghost_x.reshape(N_GX, N_GY, N_GZ, 2, 2 * GHOST)
    yz_lists = ghost_yz.reshape(N_GX, N_GY, N_GZ, 4, GHOST)
    species_f = species.astype(jnp.float32)
    packed = jnp.concatenate([positions.T, species_f[:, None]], axis=1).reshape(grid_shape + (4,))
    ghost_pack = ghosts_of(packed, x_lists, yz_lists, True).reshape(devices_n, 8 * GHOST, 4)
    own_pos = packed.reshape(devices_n, ATOMS_DEV, 4)[:, :, :3]
    zero_pos = jnp.zeros((devices_n, 1, 3), jnp.float32)
    pos_full = jnp.concatenate([own_pos, ghost_pack[:, :, :3], zero_pos], axis=1)
    one_hot = (species_f[:, None] == jnp.arange(SPECIES, dtype=jnp.float32)[None, :]).astype(jnp.float32)
    embedded = jnp.dot(one_hot, embedding.astype(jnp.float32), preferred_element_type=jnp.float32)
    owned_features = embedded.reshape(devices_n, ATOMS_DEV, MODELS * C)
    slots_dev = neighbors.reshape(NBR, devices_n, ATOMS_DEV).transpose(1, 0, 2)
    zero_feat = jnp.zeros((devices_n, 1, MODELS * C), jnp.float32)
    for layer_no in range(LAYERS):
        feat_ghost = ghosts_of(owned_features.reshape(grid_shape + (MODELS * C,)), x_lists, yz_lists, False).reshape(devices_n, 8 * GHOST, MODELS * C)
        feat_full = jnp.concatenate([owned_features, feat_ghost, zero_feat], axis=1)
        filter_w = filters[layer_no].astype(jnp.float32)
        mat_u = update_u[layer_no].astype(jnp.float32)
        mat_v = update_v[layer_no].astype(jnp.float32)

        def run_layer(member):
            return layer_dev(member, filter_w, mat_u, mat_v)

        owned_features = lax.map(run_layer, (pos_full, feat_full, slots_dev))
    head = force_w.astype(jnp.float32)

    def force_dev(member):
        pos_tab, feat_now, slot_ids, live_n = member
        displacement_vectors, radial_terms = geometry(pos_tab, slot_ids)
        basis_coefficients = jnp.einsum("amc,mck->amk", rounded(feat_now), head)
        coupling_strength = jnp.einsum("bug,glb->lug", radial_terms, basis_coefficients)
        atomic_forces = EDGE_LENGTH_SCALE * jnp.einsum("ytg,tgr->ygr", coupling_strength, displacement_vectors)
        average = jnp.mean(atomic_forces, axis=0)
        spread = jnp.mean(jnp.sum(jnp.square(atomic_forces - average[None]), axis=2), axis=0)
        alive_rows = (jnp.arange(ATOMS_DEV) < live_n).astype(jnp.float32)
        return average * alive_rows[:, None], spread * alive_rows

    average, spread = lax.map(force_dev, (pos_full, owned_features, slots_dev, atom_count))
    return average.reshape(ATOMS, 3).T, spread.reshape(ATOMS)
```

```python
import functools

import jax
import jax.numpy as jnp
from jax import lax
from jax.experimental import pallas as pl
from jax.experimental.pallas import tpu as pltpu
from jax.sharding import PartitionSpec as P

ATOMS_DEV = 256
GHOSTS = 512
TABLE = ATOMS_DEV + GHOSTS
MODELS = 4
C = 128
WIDTH = MODELS * C
KB = 8
SPECIES = 4
SLOTS_HALF = 32
SCALE = 0.125
ROOT_LOG2E = 1.2011224087864498
F32 = jnp.float32
BF16 = jnp.bfloat16
AXES = ("gx", "gy", "gz")


def iota(shape, dim):
    return lax.broadcasted_iota(jnp.int32, shape, dim)


def dot(a, b):
    return lax.dot_general(a, b, (((1,), (0,)), ((), ())), preferred_element_type=F32)


def split(x):
    high = x.astype(BF16).astype(F32)
    return high, (x - high).astype(BF16).astype(F32)


def add_silu(h, pre):
    half = 0.5 * pre
    return h + half + half * jnp.tanh(half)


def kernel(
    sizes,
    pos_ref, spec_ref, nbr_ref, live_ref, gx_ref, gyz_ref, emb_ref, filt_ref, u_hbm, v_hbm, fw_ref,
    mean_ref, dev_ref,
    sel, pack_send, pack_recv, agg_send, agg_recv, count, col, rad, left, feat, h_own, h_tab, acc,
    fbc, uvt, w_msg, w_emb, dsum, u_vm, v_vm,
    send_sem, recv_sem, copy_sem,
):
    here = [lax.axis_index(a) for a in AXES]
    peers = []
    for axis, size, me in zip(AXES, sizes, here):
        peers.append({axis: lax.rem(me + 1, size)})
        peers.append({axis: lax.rem(me + size - 1, size)})

    barrier = pltpu.get_barrier_semaphore()
    for peer in peers:
        pl.semaphore_signal(barrier, inc=1, device_id=peer, device_id_type=pl.DeviceIdType.MESH)
    u_copy = pltpu.make_async_copy(u_hbm, u_vm, copy_sem.at[0])
    v_copy = pltpu.make_async_copy(v_hbm, v_vm, copy_sem.at[1])
    u_copy.start()
    v_copy.start()

    lists = [gx_ref[0:1, :], gx_ref[1:2, :]]
    for pair in (0, 2):
        lists.append(jnp.concatenate([gyz_ref[pair : pair + 1, :], gyz_ref[pair + 1 : pair + 2, :]], axis=1))
    atom_row = iota((ATOMS_DEV, 128), 0)
    for g in range(4):
        sel[:, g * 128 : (g + 1) * 128] = jnp.where(atom_row == lists[g], 1.0, 0.0).astype(BF16)

    own = jnp.concatenate(
        [pos_ref[...], spec_ref[...].astype(F32), jnp.zeros((4, ATOMS_DEV), F32)], axis=0
    )
    high = own.astype(BF16).astype(F32)
    rest = own - high
    middle = rest.astype(BF16).astype(F32)
    low = rest - middle
    picked = dot(jnp.concatenate([high, middle, low], axis=0).astype(BF16), sel[...])
    picked = picked[0:8] + picked[8:16] + picked[16:24]
    for g in range(4):
        pack_send[g] = picked[:, g * 128 : (g + 1) * 128]

    def sends(source, target, first):
        return [
            pltpu.make_async_remote_copy(
                src_ref=source.at[group],
                dst_ref=target.at[face],
                send_sem=send_sem.at[first + face],
                recv_sem=recv_sem.at[first + face],
                device_id=peers[face],
                device_id_type=pl.DeviceIdType.MESH,
            )
            for face, group in enumerate((0, 1, 2, 2, 3, 3))
        ]

    pl.semaphore_wait(barrier, 6)
    pack_copies = sends(pack_send, pack_recv, 0)
    for c in pack_copies:
        c.start()

    def count_rows(tile, first_slot, base):
        rows = 32
        where = iota((rows, ATOMS_DEV), 0) + (tile * rows + base)
        total = jnp.zeros((rows, ATOMS_DEV), F32)
        for s in range(first_slot, first_slot + SLOTS_HALF):
            total = total + jnp.where(nbr_ref[s : s + 1, :] == where, 1.0, 0.0)
        count[pl.ds(pl.multiple_of(tile * rows + base, rows), rows), :] = total

    @pl.loop(0, ATOMS_DEV // 32)
    def _(tile):
        count_rows(tile, 0, 0)

    @pl.loop(0, GHOSTS // 32)
    def _(tile):
        count_rows(tile, SLOTS_HALF, ATOMS_DEV)

    centre = own[0:3]

    def radial_rows(tile, base):
        rows = 32
        place = pl.ds(pl.multiple_of(tile * rows + base, rows), rows)
        squared = None
        for c in range(3):
            gap = col[place, c : c + 1] - pos_ref[c : c + 1, :]
            squared = gap * gap if squared is None else squared + gap * gap
        scaled = squared * (2.0 * ROOT_LOG2E)
        times = count[place, :]
        for k in range(KB):
            off = scaled - ROOT_LOG2E * k
            rad[k, place, :] = (jnp.exp2(-(off * off)) * times).astype(BF16)

    def left_rows(packed):
        n = packed.shape[1]
        eight = iota((8, n), 0).astype(F32)
        hot_low = jnp.where(packed[3:4] == eight, 1.0, 0.0)
        hot_high = jnp.where(packed[3:4] == eight - 4.0, 1.0, 0.0)
        p_high, p_low = split(packed[0:3])
        place = jnp.concatenate([p_high, p_low, jnp.zeros((2, n), F32)], axis=0)
        blank = jnp.zeros((8, n), F32)
        even = jnp.concatenate([jnp.where(eight < 4.0, hot_low, 0.0), place, blank, blank], axis=0)
        odd = jnp.concatenate([jnp.where(eight < 4.0, 0.0, hot_high), blank, place, blank], axis=0)
        return even.astype(BF16), odd.astype(BF16), jnp.where(eight < 4.0, hot_low, 0.0)

    def gather_sums(even, odd, first, rows):
        part = []
        for q in range(4):
            part.append(
                dot(even, rad[2 * q, first : first + rows, :])
                + dot(odd, rad[2 * q + 1, first : first + rows, :])
            )
        return part

    col[0:ATOMS_DEV, :] = own.T

    @pl.loop(0, ATOMS_DEV // 32)
    def _(tile):
        radial_rows(tile, 0)

    even_own, odd_own, hot_own = left_rows(own)
    sums = gather_sums(even_own, odd_own, 0, ATOMS_DEV)

    filt = filt_ref[...].astype(F32)
    emb = emb_ref[...].astype(F32)
    emb8 = jnp.concatenate([emb, emb], axis=0)
    upper = iota((8, WIDTH), 0) < 4
    first_w = jnp.concatenate(
        [
            SCALE * emb8 * jnp.where(upper, filt[0, 2 * q : 2 * q + 1], filt[0, 2 * q + 1 : 2 * q + 2])
            for q in range(4)
        ],
        axis=0,
    )
    w_high, w_low = split(first_w)
    w_msg[...] = jnp.concatenate([w_high, w_high, w_low, jnp.zeros((32, WIDTH), F32)], axis=0).T.astype(BF16)
    w_emb[...] = jnp.concatenate(
        [jnp.zeros((96, WIDTH), F32), jnp.where(upper, emb8, 0.0), jnp.zeros((24, WIDTH), F32)], axis=0
    ).T.astype(BF16)
    filt_t = (SCALE * filt[1]).T
    for k in range(KB):
        fbc[k] = jnp.broadcast_to(filt_t[:, k : k + 1], (WIDTH, 128))
    u_copy.wait()
    v_copy.wait()
    for l in range(2):
        for m in range(MODELS):
            uvt[l, m, :, 0:128] = u_vm[l, m].astype(F32).T.astype(BF16)
            uvt[l, m, :, 128:256] = v_vm[l, m].astype(F32).T.astype(BF16)

    for c in pack_copies:
        c.wait_recv()
    lane_low = iota((8, 128), 1) < 64
    sub = iota((8, 128), 0)
    tiles = [
        pack_recv[0] - jnp.where(sub == 0, 1.0, 0.0),
        pack_recv[1] + jnp.where(sub == 0, 1.0, 0.0),
    ]
    for axis in (1, 2):
        step = jnp.where(sub == axis, 1.0, 0.0)
        tiles.append(
            jnp.where(lane_low, pack_recv[2 * axis] - step, pack_recv[2 * axis + 1] + step)
        )
    lent = jnp.concatenate(tiles, axis=1)
    col[ATOMS_DEV:TABLE, :] = lent.T

    @pl.loop(0, GHOSTS // 32)
    def _(tile):
        radial_rows(tile, ATOMS_DEV)

    even_lent, odd_lent, hot_lent = left_rows(lent)
    more = gather_sums(even_lent, odd_lent, ATOMS_DEV, GHOSTS)
    sums = [a + b for a, b in zip(sums, more)]

    agg = jnp.concatenate([s[0:8] for s in sums], axis=0)
    a_high, a_low = split(agg)
    chosen = dot(jnp.concatenate([a_high, a_low], axis=0).astype(BF16), sel[...])
    chosen = chosen[0:32] + chosen[32:64]
    for g in range(4):
        agg_send[g] = chosen[:, g * 128 : (g + 1) * 128]
    agg_copies = sends(agg_send, agg_recv, 6)
    for c in agg_copies:
        c.start()

    for q in range(4):
        for odd in range(2):
            k = 2 * q + odd
            weight = jnp.sum(sums[q][4 * odd : 4 * odd + 4], axis=0, keepdims=True)
            base = 8 + 8 * odd
            for c in range(3):
                dsum[c, k : k + 1, :] = (
                    sums[q][base + c : base + c + 1]
                    + sums[q][base + 3 + c : base + 4 + c]
                    - centre[c : c + 1] * weight
                )

    def first_layer(table, hot):
        n = table.shape[1]
        t_high, t_low = split(table)
        x = jnp.concatenate([t_high, t_low, t_high, hot, jnp.zeros((24, n), F32)], axis=0).astype(BF16)
        result = []
        for m in range(MODELS):
            rows = slice(m * C, (m + 1) * C)
            msg = dot(w_msg[rows, :], x).astype(BF16)
            h = dot(w_emb[rows, :], x)
            pre = dot(uvt[0, m], jnp.concatenate([msg, h.astype(BF16)], axis=0))
            result.append(add_silu(h, pre))
        return result

    for m, h in enumerate(first_layer(agg, hot_own)):
        h_own[m * C : (m + 1) * C, :] = h
        h_tab[m * C : (m + 1) * C, 0:ATOMS_DEV] = h.astype(BF16)

    def second_messages(first, rows, begin):
        for k in range(KB):
            part = dot(h_tab[:, first : first + rows], rad[k, first : first + rows, :])
            for half in range(2):
                lanes = slice(half * 128, (half + 1) * 128)
                scaled = fbc[k] * part[:, lanes]
                acc[:, lanes] = scaled if begin and k == 0 else acc[:, lanes] + scaled

    second_messages(0, ATOMS_DEV, True)

    for c in agg_copies:
        c.wait_recv()
    wide_low = iota((32, 128), 1) < 64
    tables = [agg_recv[0], agg_recv[1]]
    for axis in (1, 2):
        tables.append(jnp.where(wide_low, agg_recv[2 * axis], agg_recv[2 * axis + 1]))
    for m, h in enumerate(first_layer(jnp.concatenate(tables, axis=1), hot_lent)):
        h_tab[m * C : (m + 1) * C, ATOMS_DEV:TABLE] = h.astype(BF16)
    second_messages(ATOMS_DEV, GHOSTS, False)

    forces = []
    for m in range(MODELS):
        rows = slice(m * C, (m + 1) * C)
        x = jnp.concatenate([acc[rows, :].astype(BF16), h_tab[rows, 0:ATOMS_DEV]], axis=0)
        h = add_silu(h_own[rows, :], dot(uvt[1, m], x))
        coeff = dot(fw_ref[m], h.astype(BF16))
        forces.append([SCALE * jnp.sum(coeff * dsum[c], axis=0, keepdims=True) for c in range(3)])
    alive = jnp.where(iota((1, ATOMS_DEV), 1) < live_ref[...], 1.0, 0.0)
    spread = jnp.zeros((1, ATOMS_DEV), F32)
    for c in range(3):
        mean = (forces[0][c] + forces[1][c] + forces[2][c] + forces[3][c]) * 0.25
        for m in range(MODELS):
            gap = forces[m][c] - mean
            spread = spread + gap * gap
        mean_ref[c : c + 1, :] = mean * alive
    dev_ref[...] = spread * 0.25 * alive

    for c in pack_copies + agg_copies:
        c.wait_send()


def solution(mesh):
    sizes = tuple(mesh.shape[a] for a in AXES)

    def local(positions, species, neighbors, atom_count, ghost_x, ghost_yz, embedding, filters, update_u, update_v, force_w):
        vmem = pl.BlockSpec(memory_space=pltpu.VMEM)
        anywhere = pl.BlockSpec(memory_space=pl.ANY)
        mean, spread = pl.pallas_call(
            functools.partial(kernel, sizes),
            out_shape=(
                jax.ShapeDtypeStruct((3, ATOMS_DEV), F32),
                jax.ShapeDtypeStruct((1, ATOMS_DEV), F32),
            ),
            in_specs=[vmem, vmem, vmem, vmem, vmem, vmem, vmem, vmem, anywhere, anywhere, vmem],
            out_specs=(vmem, vmem),
            scratch_shapes=[
                pltpu.VMEM((ATOMS_DEV, GHOSTS), BF16),
                pltpu.VMEM((4, 8, 128), F32),
                pltpu.VMEM((6, 8, 128), F32),
                pltpu.VMEM((4, 32, 128), F32),
                pltpu.VMEM((6, 32, 128), F32),
                pltpu.VMEM((TABLE, ATOMS_DEV), F32),
                pltpu.VMEM((TABLE, 8), F32),
                pltpu.VMEM((KB, TABLE, ATOMS_DEV), BF16),
                pltpu.VMEM((8, 128), F32),
                pltpu.VMEM((8, 128), F32),
                pltpu.VMEM((WIDTH, ATOMS_DEV), F32),
                pltpu.VMEM((WIDTH, TABLE), BF16),
                pltpu.VMEM((WIDTH, ATOMS_DEV), F32),
                pltpu.VMEM((KB, WIDTH, 128), F32),
                pltpu.VMEM((2, MODELS, C, 2 * C), BF16),
                pltpu.VMEM((WIDTH, 128), BF16),
                pltpu.VMEM((WIDTH, 128), BF16),
                pltpu.VMEM((3, KB, ATOMS_DEV), F32),
                pltpu.VMEM((2, MODELS, C, C), BF16),
                pltpu.VMEM((2, MODELS, C, C), BF16),
                pltpu.SemaphoreType.DMA((12,)),
                pltpu.SemaphoreType.DMA((12,)),
                pltpu.SemaphoreType.DMA((2,)),
            ],
            compiler_params=pltpu.CompilerParams(
                collective_id=0, has_side_effects=True, vmem_limit_bytes=60 * 1024 * 1024
            ),
        )(
            positions,
            species.reshape(1, ATOMS_DEV),
            neighbors,
            atom_count.reshape(1, 1),
            ghost_x.reshape(2, 2 * 64),
            ghost_yz.reshape(4, 64),
            embedding,
            filters,
            update_u,
            update_v,
            jnp.swapaxes(force_w, 1, 2),
        )
        return mean, spread.reshape(ATOMS_DEV)

    split_spec = P(AXES)
    return jax.shard_map(
        local,
        mesh=mesh,
        in_specs=(
            P(None, AXES), split_spec, P(None, AXES), split_spec,
            P(AXES, None, None), P(AXES, None, None), P(), P(), P(), P(), P(),
        ),
        out_specs=(P(None, AXES), split_spec),
        check_vma=False,
    )
```

```python
import functools

import jax
import jax.numpy as jnp
from jax import lax
from jax.experimental import pallas as pl
from jax.experimental.pallas import tpu as pltpu
from jax.sharding import PartitionSpec as P

ATOMS_DEV = 256
GHOSTS = 512
TABLE = ATOMS_DEV + GHOSTS
MODELS = 4
C = 128
WIDTH = MODELS * C
KB = 8
SPECIES = 4
SLOTS_HALF = 32
SCALE = 0.125
ROOT_LOG2E = 1.2011224087864498
F32 = jnp.float32
BF16 = jnp.bfloat16
AXES = ("gx", "gy", "gz")


def iota(shape, dim):
    return lax.broadcasted_iota(jnp.int32, shape, dim)


def dot(a, b):
    return lax.dot_general(a, b, (((1,), (0,)), ((), ())), preferred_element_type=F32)


def split(x):
    high = x.astype(BF16).astype(F32)
    return high, (x - high).astype(BF16).astype(F32)


def add_silu(h, pre):
    half = 0.5 * pre
    return h + half + half * jnp.tanh(half)


LOG2E = 1.4426950408889634
DROP = 0.1353352832366127


def kernel(
    sizes,
    pos_hbm, spec_hbm, nbr_hbm, live_hbm, gx_hbm, gyz_hbm, emb_ref, filt_ref, u_hbm, v_hbm, fw_ref,
    mean_ref, dev_ref,
    pos_ref, spec_ref, nbr_ref, live_ref, gx_ref, gyz_ref, u_vm, v_vm,
    sel, pack_send, pack_recv, agg_send, agg_recv, slots, count, col, rad, h_own, h_tab, acc,
    fbc, uvt, w_msg, w_emb, dsum, sent,
    send_sem, recv_sem, copy_sem,
):
    here = [lax.axis_index(a) for a in AXES]
    odd_x = lax.rem(here[0], 2)
    step_x = 1 - 2 * odd_x
    def peer(number, step):
        size = sizes[number]
        return {AXES[number]: lax.rem(here[number] + step + size, size)}

    peers = [peer(2, 1), peer(2, -1), peer(0, step_x), peer(0, -step_x), peer(1, 1), peer(1, -1)]

    barrier = pltpu.get_barrier_semaphore()
    for target in peers:
        pl.semaphore_signal(barrier, inc=1, device_id=target, device_id_type=pl.DeviceIdType.MESH)
    loads = [
        pltpu.make_async_copy(source, target, copy_sem.at[n])
        for n, (source, target) in enumerate(
            (
                (gx_hbm, gx_ref), (gyz_hbm, gyz_ref), (pos_hbm, pos_ref), (spec_hbm, spec_ref),
                (nbr_hbm, nbr_ref), (u_hbm, u_vm), (v_hbm, v_vm), (live_hbm, live_ref),
            )
        )
    ]
    for c in loads:
        c.start()
    for c in loads[0:4]:
        c.wait()

    lists = [
        jnp.concatenate([gyz_ref[2:3, :], gyz_ref[3:4, :]], axis=1),
        gx_ref[pl.ds(odd_x, 1), :],
        gx_ref[pl.ds(1 - odd_x, 1), :],
        jnp.concatenate([gyz_ref[0:1, :], gyz_ref[1:2, :]], axis=1),
    ]
    atom_row = iota((ATOMS_DEV, 128), 0)
    for g in range(4):
        sel[:, g * 128 : (g + 1) * 128] = jnp.where(atom_row == lists[g], 1.0, 0.0).astype(BF16)

    own = jnp.concatenate(
        [pos_ref[...], spec_ref[...].astype(F32), jnp.zeros((4, ATOMS_DEV), F32)], axis=0
    )
    high = own.astype(BF16).astype(F32)
    rest = own - high
    middle = rest.astype(BF16).astype(F32)
    low = rest - middle
    picked = dot(jnp.concatenate([high, middle, low], axis=0).astype(BF16), sel[...])
    picked = picked[0:8] + picked[8:16] + picked[16:24]
    for g in range(4):
        pack_send[g] = picked[:, g * 128 : (g + 1) * 128]

    def sends(source, target, first):
        return [
            pltpu.make_async_remote_copy(
                src_ref=source.at[group],
                dst_ref=target.at[face],
                send_sem=send_sem.at[first + face],
                recv_sem=recv_sem.at[first + face],
                device_id=peers[face],
                device_id_type=pl.DeviceIdType.MESH,
            )
            for face, group in enumerate((0, 0, 1, 2, 3, 3))
        ]

    pl.semaphore_wait(barrier, 6)
    pack_copies = sends(pack_send, pack_recv, 0)
    for n in (3, 4, 5, 0, 1, 2):
        pack_copies[n].start()

    loads[4].wait()
    for s in range(SLOTS_HALF):
        slots[s] = jnp.broadcast_to(nbr_ref[s : s + 1, :].astype(F32), (16, ATOMS_DEV)).astype(BF16)
        lent_id = jnp.broadcast_to(nbr_ref[SLOTS_HALF + s : SLOTS_HALF + s + 1, :].astype(F32), (16, ATOMS_DEV))
        slots[SLOTS_HALF + s] = (lent_id - 256.0).astype(BF16)
        slots[2 * SLOTS_HALF + s] = (lent_id - 512.0).astype(BF16)

    one = jnp.ones((16, ATOMS_DEV), BF16)
    nil = jnp.zeros((16, ATOMS_DEV), BF16)

    def count_rows(first_slot, base, first_row, rows):
        @pl.loop(0, rows // 64)
        def _(tile):
            which = [
                (iota((16, ATOMS_DEV), 0) + (tile * 64 + base + 16 * r)).astype(F32).astype(BF16)
                for r in range(4)
            ]
            total = [nil] * 4
            for s in range(first_slot, first_slot + SLOTS_HALF):
                ids = slots[s]
                total = [t + jnp.where(ids == w, one, nil) for t, w in zip(total, which)]
            for r in range(4):
                place = pl.ds(pl.multiple_of(tile * 64 + (first_row + 16 * r), 16), 16)
                count[place, :] = total[r]

    count_rows(0, 0, 0, 256)
    count_rows(2 * SLOTS_HALF, 128, 256, 128)
    count_rows(SLOTS_HALF, 128 * (1 - odd_x), 384, 128)
    count_rows(SLOTS_HALF, 128 * odd_x, 512, 128)
    count_rows(2 * SLOTS_HALF, 0, 640, 128)

    centre = own[0:3]

    def radial_rows(part):
        rows = 32
        for tile in range(256 // rows):
            first = part * 256 + tile * rows
            squared = None
            for c in range(3):
                gap = col[first : first + rows, c : c + 1] - pos_ref[c : c + 1, :]
                squared = gap * gap if squared is None else squared + gap * gap
            off = squared * (2.0 * ROOT_LOG2E) - 4.0 * ROOT_LOG2E
            grow = squared * (4.0 * LOG2E)
            up = jnp.exp2(grow - 9.0 * LOG2E)
            down = jnp.exp2(7.0 * LOG2E - grow)
            mid = jnp.exp2(-(off * off)) * count[first : first + rows, :].astype(F32)

            def put(k, value):
                rad[part, k * 256 + tile * rows : k * 256 + (tile + 1) * rows, :] = value.astype(BF16)

            put(4, mid)
            value = mid
            for k in (5, 6, 7):
                value = value * up
                put(k, value)
                up = up * DROP
            value = mid
            for k in (3, 2, 1, 0):
                value = value * down
                put(k, value)
                down = down * DROP

    def left_rows(packed):
        n = packed.shape[1]
        eight = iota((8, n), 0).astype(F32)
        hot = jnp.where(packed[3:4] == eight, 1.0, 0.0)
        hot_high = jnp.where(packed[3:4] == eight - 4.0, 1.0, 0.0)
        p_high, p_low = split(packed[0:3])
        place = jnp.concatenate([p_high, p_low, jnp.zeros((2, n), F32)], axis=0)
        blank = jnp.zeros((8, n), F32)
        even = jnp.concatenate([hot, place, blank, blank], axis=0)
        odd = jnp.concatenate([hot_high, blank, place, blank], axis=0)
        return jnp.concatenate([even.astype(BF16), odd.astype(BF16)], axis=1), hot

    def gather_sums(both, part):
        return [dot(both, rad[part, q * 512 : (q + 1) * 512, :]) for q in range(4)]

    col[0:256, :] = own.T
    radial_rows(0)
    both_own, hot_own = left_rows(own)
    for q, s in enumerate(gather_sums(both_own, 0)):
        sent[q] = s

    filt = filt_ref[...].astype(F32)
    emb = emb_ref[...].astype(F32)
    emb8 = jnp.concatenate([emb, emb], axis=0)
    upper = iota((8, WIDTH), 0) < 4
    first_w = jnp.concatenate(
        [
            SCALE * emb8 * jnp.where(upper, filt[0, 2 * q : 2 * q + 1], filt[0, 2 * q + 1 : 2 * q + 2])
            for q in range(4)
        ],
        axis=0,
    )
    w_high, w_low = split(first_w)
    w_msg[...] = jnp.concatenate([w_high, w_high, w_low, jnp.zeros((32, WIDTH), F32)], axis=0).T.astype(BF16)
    w_emb[...] = jnp.concatenate(
        [jnp.zeros((96, WIDTH), F32), jnp.where(upper, emb8, 0.0), jnp.zeros((24, WIDTH), F32)], axis=0
    ).T.astype(BF16)
    filt_t = (SCALE * filt[1]).T
    for k in range(KB):
        fbc[k] = jnp.broadcast_to(filt_t[:, k : k + 1], (WIDTH, 128)).astype(BF16)
    loads[5].wait()
    loads[6].wait()
    for l in range(2):
        for m in range(MODELS):
            uvt[l, m, :, 0:128] = u_vm[l, m].astype(F32).T.astype(BF16)
            uvt[l, m, :, 128:256] = v_vm[l, m].astype(F32).T.astype(BF16)

    lane_low = iota((8, 128), 1) < 64
    sub = iota((8, 128), 0)

    def pair(first, axis):
        step = jnp.where(sub == axis, 1.0, 0.0)
        return jnp.where(lane_low, pack_recv[first] - step, pack_recv[first + 1] + step)

    near = jnp.where(sub == 0, step_x.astype(F32), 0.0)
    for c in pack_copies[0:3]:
        c.wait_recv()
    early = jnp.concatenate([pair(0, 2), pack_recv[2] + near], axis=1)
    col[256:512, :] = early.T
    radial_rows(1)
    both_early, hot_early = left_rows(early)
    for q, s in enumerate(gather_sums(both_early, 1)):
        sent[q] = sent[q] + s

    for c in pack_copies[3:6]:
        c.wait_recv()
    late = jnp.concatenate([pack_recv[3] - near, pair(4, 1)], axis=1)
    col[512:768, :] = late.T
    radial_rows(2)
    both_late, hot_late = left_rows(late)
    sums = [sent[q] + s for q, s in enumerate(gather_sums(both_late, 2))]

    agg = jnp.concatenate([s[0:8] for s in sums], axis=0)
    a_high, a_low = split(agg)
    chosen = dot(jnp.concatenate([a_high, a_low], axis=0).astype(BF16), sel[...])
    chosen = chosen[0:32] + chosen[32:64]
    for g in range(4):
        agg_send[g] = chosen[:, g * 128 : (g + 1) * 128]
    agg_copies = sends(agg_send, agg_recv, 6)
    for n in (3, 4, 5, 0, 1, 2):
        agg_copies[n].start()

    for q in range(4):
        for odd in range(2):
            k = 2 * q + odd
            weight = jnp.sum(sums[q][4 * odd : 4 * odd + 4], axis=0, keepdims=True)
            base = 8 + 8 * odd
            for c in range(3):
                dsum[c, k : k + 1, :] = (
                    sums[q][base + c : base + c + 1]
                    + sums[q][base + 3 + c : base + 4 + c]
                    - centre[c : c + 1] * weight
                )

    def first_layer(table, hot):
        n = table.shape[1]
        t_high, t_low = split(table)
        x = jnp.concatenate([t_high, t_low, t_high, hot, jnp.zeros((24, n), F32)], axis=0).astype(BF16)
        result = []
        for m in range(MODELS):
            rows = slice(m * C, (m + 1) * C)
            msg = dot(w_msg[rows, :], x).astype(BF16)
            h = dot(w_emb[rows, :], x)
            pre = dot(uvt[0, m], jnp.concatenate([msg, h.astype(BF16)], axis=0))
            result.append(add_silu(h, pre))
        return result

    def weigh(m, h):
        rows = slice(m * C, (m + 1) * C)
        for k in range(KB):
            for half in range(2):
                lanes = slice(half * 128, (half + 1) * 128)
                h_tab[rows, k * 256 + half * 128 : k * 256 + (half + 1) * 128] = h[:, lanes] * fbc[k, rows, :]

    for m, h in enumerate(first_layer(agg, hot_own)):
        h_own[m * C : (m + 1) * C, :] = h
        weigh(m, h.astype(BF16))
    acc[...] = dot(h_tab[...], rad[0])

    wide_low = iota((32, 128), 1) < 64

    def agg_pair(first):
        return jnp.where(wide_low, agg_recv[first], agg_recv[first + 1])

    for c in agg_copies[0:3]:
        c.wait_recv()
    for m, h in enumerate(first_layer(jnp.concatenate([agg_pair(0), agg_recv[2]], axis=1), hot_early)):
        weigh(m, h.astype(BF16))
    acc[...] += dot(h_tab[...], rad[1])
    for c in agg_copies[3:6]:
        c.wait_recv()
    for m, h in enumerate(first_layer(jnp.concatenate([agg_recv[3], agg_pair(4)], axis=1), hot_late)):
        weigh(m, h.astype(BF16))
    message = (acc[...] + dot(h_tab[...], rad[2])).astype(BF16)

    forces = []
    for m in range(MODELS):
        rows = slice(m * C, (m + 1) * C)
        x = jnp.concatenate([message[rows], h_own[rows, :].astype(BF16)], axis=0)
        h = add_silu(h_own[rows, :], dot(uvt[1, m], x))
        coeff = dot(fw_ref[m], h.astype(BF16))
        forces.append([SCALE * jnp.sum(coeff * dsum[c], axis=0, keepdims=True) for c in range(3)])
    loads[7].wait()
    alive = jnp.where(iota((1, ATOMS_DEV), 1) < live_ref[...], 1.0, 0.0)
    spread = jnp.zeros((1, ATOMS_DEV), F32)
    for c in range(3):
        mean = (forces[0][c] + forces[1][c] + forces[2][c] + forces[3][c]) * 0.25
        for m in range(MODELS):
            gap = forces[m][c] - mean
            spread = spread + gap * gap
        mean_ref[c : c + 1, :] = mean * alive
    dev_ref[...] = spread * 0.25 * alive

    for c in pack_copies + agg_copies:
        c.wait_send()


def solution(mesh):
    sizes = tuple(mesh.shape[a] for a in AXES)

    def local(positions, species, neighbors, atom_count, ghost_x, ghost_yz, embedding, filters, update_u, update_v, force_w):
        vmem = pl.BlockSpec(memory_space=pltpu.VMEM)
        anywhere = pl.BlockSpec(memory_space=pl.ANY)
        mean, spread = pl.pallas_call(
            functools.partial(kernel, sizes),
            out_shape=(pltpu.VMEM((3, ATOMS_DEV), F32), pltpu.VMEM((1, ATOMS_DEV), F32)),
            in_specs=[anywhere] * 6 + [vmem, vmem, anywhere, anywhere, vmem],
            out_specs=(vmem, vmem),
            scratch_shapes=[
                pltpu.VMEM((3, ATOMS_DEV), F32),
                pltpu.VMEM((1, ATOMS_DEV), jnp.int32),
                pltpu.VMEM((2 * SLOTS_HALF, ATOMS_DEV), jnp.int32),
                pltpu.VMEM((1, 1), jnp.int32),
                pltpu.VMEM((2, 128), jnp.int32),
                pltpu.VMEM((4, 64), jnp.int32),
                pltpu.VMEM((2, MODELS, C, C), BF16),
                pltpu.VMEM((2, MODELS, C, C), BF16),
                pltpu.VMEM((ATOMS_DEV, GHOSTS), BF16),
                pltpu.VMEM((4, 8, 128), F32),
                pltpu.VMEM((6, 8, 128), F32),
                pltpu.VMEM((4, 32, 128), F32),
                pltpu.VMEM((6, 32, 128), F32),
                pltpu.VMEM((3 * SLOTS_HALF, 16, ATOMS_DEV), BF16),
                pltpu.VMEM((TABLE, ATOMS_DEV), BF16),
                pltpu.VMEM((TABLE, 8), F32),
                pltpu.VMEM((3, KB * 256, ATOMS_DEV), BF16),
                pltpu.VMEM((WIDTH, ATOMS_DEV), F32),
                pltpu.VMEM((WIDTH, KB * 256), BF16),
                pltpu.VMEM((WIDTH, ATOMS_DEV), F32),
                pltpu.VMEM((KB, WIDTH, 128), BF16),
                pltpu.VMEM((2, MODELS, C, 2 * C), BF16),
                pltpu.VMEM((WIDTH, 128), BF16),
                pltpu.VMEM((WIDTH, 128), BF16),
                pltpu.VMEM((3, KB, ATOMS_DEV), F32),
                pltpu.VMEM((4, 32, ATOMS_DEV), F32),
                pltpu.SemaphoreType.DMA((12,)),
                pltpu.SemaphoreType.DMA((12,)),
                pltpu.SemaphoreType.DMA((8,)),
            ],
            compiler_params=pltpu.CompilerParams(
                collective_id=0, has_side_effects=True, vmem_limit_bytes=60 * 1024 * 1024
            ),
        )(
            positions,
            species.reshape(1, ATOMS_DEV),
            neighbors,
            atom_count.reshape(1, 1),
            ghost_x.reshape(2, 2 * 64),
            ghost_yz.reshape(4, 64),
            embedding,
            filters,
            update_u,
            update_v,
            jnp.swapaxes(force_w, 1, 2),
        )
        return mean, spread.reshape(ATOMS_DEV)

    split_spec = P(AXES)
    return jax.shard_map(
        local,
        mesh=mesh,
        in_specs=(
            P(None, AXES), split_spec, P(None, AXES), split_spec,
            P(AXES, None, None), P(AXES, None, None), P(), P(), P(), P(), P(),
        ),
        out_specs=(P(None, AXES), split_spec),
        check_vma=False,
    )
```

```python
import functools

import jax
import jax.numpy as jnp
from jax import lax
from jax.experimental import pallas as pl
from jax.experimental.pallas import tpu as pltpu
from jax.sharding import PartitionSpec as P

ATOMS_DEV = 256
GHOSTS = 512
TABLE = ATOMS_DEV + GHOSTS
MODELS = 4
C = 128
WIDTH = MODELS * C
KB = 8
SPECIES = 4
SLOTS_HALF = 32
SCALE = 0.125
ROOT_LOG2E = 1.2011224087864498
F32 = jnp.float32
BF16 = jnp.bfloat16
AXES = ("gx", "gy", "gz")


def iota(shape, dim):
    return lax.broadcasted_iota(jnp.int32, shape, dim)


def dot(a, b):
    return lax.dot_general(a, b, (((1,), (0,)), ((), ())), preferred_element_type=F32)


def split(x):
    high = x.astype(BF16).astype(F32)
    return high, (x - high).astype(BF16).astype(F32)


def add_silu(h, pre):
    half = 0.5 * pre
    return h + half + half * jnp.tanh(half)


LOG2E = 1.4426950408889634
DROP = 0.1353352832366127


def kernel(
    sizes,
    pos_hbm, spec_hbm, nbr_hbm, live_hbm, gx_hbm, gyz_hbm, emb_hbm, filt_hbm, u_hbm, v_hbm, fw_hbm,
    mean_ref, dev_ref,
    pos_ref, spec_ref, nbr_ref, live_ref, gx_ref, gyz_ref, u_vm, v_vm, emb_ref, filt_ref, fw_ref,
    sel, pack_send, pack_recv, agg_send, agg_recv, slots, count, col, rad, h_own, h_tab, acc,
    fbc, uvt, w_msg, dsum, sent,
    send_sem, recv_sem, copy_sem,
):
    here = [lax.axis_index(a) for a in AXES]
    odd_x = lax.rem(here[0], 2)
    step_x = 1 - 2 * odd_x
    def peer(number, step):
        size = sizes[number]
        return {AXES[number]: lax.rem(here[number] + step + size, size)}

    peers = [peer(2, 1), peer(2, -1), peer(0, step_x), peer(0, -step_x), peer(1, 1), peer(1, -1)]

    barrier = pltpu.get_barrier_semaphore()
    for target in peers:
        pl.semaphore_signal(barrier, inc=1, device_id=target, device_id_type=pl.DeviceIdType.MESH)
    loads = [
        pltpu.make_async_copy(source, target, copy_sem.at[n])
        for n, (source, target) in enumerate(
            (
                (gx_hbm, gx_ref), (gyz_hbm, gyz_ref), (pos_hbm, pos_ref), (spec_hbm, spec_ref),
                (nbr_hbm, nbr_ref), (emb_hbm, emb_ref), (filt_hbm, filt_ref), (u_hbm, u_vm), (v_hbm, v_vm), (fw_hbm, fw_ref), (live_hbm, live_ref),
            )
        )
    ]
    for c in loads:
        c.start()
    for c in loads[0:4]:
        c.wait()

    lists = [
        jnp.concatenate([gyz_ref[2:3, :], gyz_ref[3:4, :]], axis=1),
        gx_ref[pl.ds(odd_x, 1), :],
        gx_ref[pl.ds(1 - odd_x, 1), :],
        jnp.concatenate([gyz_ref[0:1, :], gyz_ref[1:2, :]], axis=1),
    ]
    atom_row = iota((ATOMS_DEV, 128), 0)
    for g in range(4):
        sel[:, g * 128 : (g + 1) * 128] = jnp.where(atom_row == lists[g], 1.0, 0.0).astype(BF16)

    own = jnp.concatenate(
        [pos_ref[...], spec_ref[...].astype(F32), jnp.zeros((4, ATOMS_DEV), F32)], axis=0
    )
    high = own.astype(BF16).astype(F32)
    rest = own - high
    middle = rest.astype(BF16).astype(F32)
    low = rest - middle
    picked = dot(jnp.concatenate([high, middle, low], axis=0).astype(BF16), sel[...])
    picked = picked[0:8] + picked[8:16] + picked[16:24]
    for g in range(4):
        pack_send[g] = picked[:, g * 128 : (g + 1) * 128]

    def sends(source, target, first):
        return [
            pltpu.make_async_remote_copy(
                src_ref=source.at[group],
                dst_ref=target.at[face],
                send_sem=send_sem.at[first + face],
                recv_sem=recv_sem.at[first + face],
                device_id=peers[face],
                device_id_type=pl.DeviceIdType.MESH,
            )
            for face, group in enumerate((0, 0, 1, 2, 3, 3))
        ]

    pl.semaphore_wait(barrier, 6)
    pack_copies = sends(pack_send, pack_recv, 0)
    for n in (3, 4, 5, 0, 1, 2):
        pack_copies[n].start()

    loads[4].wait()
    for s in range(SLOTS_HALF):
        slots[s] = jnp.broadcast_to(nbr_ref[s : s + 1, :].astype(F32), (16, ATOMS_DEV)).astype(BF16)
        lent_id = jnp.broadcast_to(nbr_ref[SLOTS_HALF + s : SLOTS_HALF + s + 1, :].astype(F32), (16, ATOMS_DEV))
        slots[SLOTS_HALF + s] = (lent_id - 256.0).astype(BF16)
        slots[2 * SLOTS_HALF + s] = (lent_id - 512.0).astype(BF16)

    one = jnp.ones((16, ATOMS_DEV), BF16)
    nil = jnp.zeros((16, ATOMS_DEV), BF16)

    def count_rows(first_slot, base, first_row, rows):
        @pl.loop(0, rows // 64)
        def _(tile):
            which = [
                (iota((16, ATOMS_DEV), 0) + (tile * 64 + base + 16 * r)).astype(F32).astype(BF16)
                for r in range(4)
            ]
            total = [nil] * 4
            for s in range(first_slot, first_slot + SLOTS_HALF):
                ids = slots[s]
                total = [t + jnp.where(ids == w, one, nil) for t, w in zip(total, which)]
            for r in range(4):
                place = pl.ds(pl.multiple_of(tile * 64 + (first_row + 16 * r), 16), 16)
                count[place, :] = total[r]

    count_rows(0, 0, 0, 256)
    count_rows(2 * SLOTS_HALF, 128, 256, 128)
    count_rows(SLOTS_HALF, 128 * (1 - odd_x), 384, 128)
    count_rows(SLOTS_HALF, 128 * odd_x, 512, 128)
    count_rows(2 * SLOTS_HALF, 0, 640, 128)

    centre = own[0:3]

    def radial_rows(part):
        rows = 32
        for tile in range(256 // rows):
            first = part * 256 + tile * rows
            squared = None
            for c in range(3):
                gap = col[first : first + rows, c : c + 1] - pos_ref[c : c + 1, :]
                squared = gap * gap if squared is None else squared + gap * gap
            off = squared * (2.0 * ROOT_LOG2E) - 4.0 * ROOT_LOG2E
            grow = squared * (4.0 * LOG2E)
            up = jnp.exp2(grow - 9.0 * LOG2E)
            down = jnp.exp2(7.0 * LOG2E - grow)
            mid = jnp.exp2(-(off * off)) * count[first : first + rows, :].astype(F32)

            def put(k, value):
                rad[part, k * 256 + tile * rows : k * 256 + (tile + 1) * rows, :] = value.astype(BF16)

            put(4, mid)
            value = mid
            for k in (5, 6, 7):
                value = value * up
                put(k, value)
                up = up * DROP
            value = mid
            for k in (3, 2, 1, 0):
                value = value * down
                put(k, value)
                down = down * DROP

    def left_rows(packed):
        n = packed.shape[1]
        eight = iota((8, n), 0).astype(F32)
        hot = jnp.where(packed[3:4] == eight, 1.0, 0.0)
        hot_high = jnp.where(packed[3:4] == eight - 4.0, 1.0, 0.0)
        p_high, p_low = split(packed[0:3])
        place = jnp.concatenate([p_high, p_low, jnp.zeros((2, n), F32)], axis=0)
        blank = jnp.zeros((8, n), F32)
        even = jnp.concatenate([hot, place, blank, blank], axis=0)
        odd = jnp.concatenate([hot_high, blank, place, blank], axis=0)
        return jnp.concatenate([even.astype(BF16), odd.astype(BF16)], axis=1), hot

    def gather_sums(both, part):
        return [dot(both, rad[part, q * 512 : (q + 1) * 512, :]) for q in range(4)]

    col[0:256, :] = own.T
    radial_rows(0)
    both_own, hot_own = left_rows(own)
    for q, s in enumerate(gather_sums(both_own, 0)):
        sent[q] = s

    lane_low = iota((8, 128), 1) < 64
    sub = iota((8, 128), 0)

    def pair(first, axis):
        step = jnp.where(sub == axis, 1.0, 0.0)
        return jnp.where(lane_low, pack_recv[first] - step, pack_recv[first + 1] + step)

    near = jnp.where(sub == 0, step_x.astype(F32), 0.0)
    for c in pack_copies[0:3]:
        c.wait_recv()
    early = jnp.concatenate([pair(0, 2), pack_recv[2] + near], axis=1)
    col[256:512, :] = early.T
    radial_rows(1)
    both_early, hot_early = left_rows(early)
    for q, s in enumerate(gather_sums(both_early, 1)):
        sent[q] = sent[q] + s

    for c in pack_copies[3:6]:
        c.wait_recv()
    late = jnp.concatenate([pack_recv[3] - near, pair(4, 1)], axis=1)
    col[512:768, :] = late.T
    radial_rows(2)
    both_late, hot_late = left_rows(late)
    sums = [sent[q] + s for q, s in enumerate(gather_sums(both_late, 2))]

    agg = jnp.concatenate([s[0:8] for s in sums], axis=0)
    a_high, a_low = split(agg)
    chosen = dot(jnp.concatenate([a_high, a_low], axis=0).astype(BF16), sel[...])
    chosen = chosen[0:32] + chosen[32:64]
    for g in range(4):
        agg_send[g] = chosen[:, g * 128 : (g + 1) * 128]
    agg_copies = sends(agg_send, agg_recv, 6)
    for n in (3, 4, 5, 0, 1, 2):
        agg_copies[n].start()

    loads[5].wait()
    loads[6].wait()
    filt = filt_ref[...].astype(F32)
    emb = emb_ref[...].astype(F32)
    emb8 = jnp.concatenate([emb, emb], axis=0)
    upper = iota((8, WIDTH), 0) < 4
    first_w = jnp.concatenate(
        [
            SCALE * emb8 * jnp.where(upper, filt[0, 2 * q : 2 * q + 1], filt[0, 2 * q + 1 : 2 * q + 2])
            for q in range(4)
        ],
        axis=0,
    )
    w_high, w_low = split(first_w)
    w_msg[...] = jnp.concatenate([w_high, w_high, w_low, jnp.where(upper, emb8, 0.0), SCALE * filt[1], jnp.zeros((16, WIDTH), F32)], axis=0).T.astype(BF16)
    for k in range(KB):
        ones = jnp.where(iota((128, 128), 0) == 104 + k, 1.0, 0.0).astype(BF16)
        fbc[k] = dot(w_msg[...], ones).astype(BF16)
    loads[7].wait()
    loads[8].wait()
    for l in range(2):
        for m in range(MODELS):
            uvt[l, m, :, 0:128] = u_vm[l, m].astype(F32).T.astype(BF16)
            uvt[l, m, :, 128:256] = v_vm[l, m].astype(F32).T.astype(BF16)

    for q in range(4):
        for odd in range(2):
            k = 2 * q + odd
            weight = jnp.sum(sums[q][4 * odd : 4 * odd + 4], axis=0, keepdims=True)
            base = 8 + 8 * odd
            for c in range(3):
                dsum[c, k : k + 1, :] = (
                    sums[q][base + c : base + c + 1]
                    + sums[q][base + 3 + c : base + 4 + c]
                    - centre[c : c + 1] * weight
                )

    def first_layer(table, hot):
        n = table.shape[1]
        t_high, t_low = split(table)
        blank = jnp.zeros((32, n), F32)
        x = jnp.concatenate([t_high, t_low, t_high, blank], axis=0).astype(BF16)
        z = jnp.concatenate([blank, blank, blank, hot, blank[0:24]], axis=0).astype(BF16)
        result = []
        for m in range(MODELS):
            rows = slice(m * C, (m + 1) * C)
            msg = dot(w_msg[rows, :], x).astype(BF16)
            h = dot(w_msg[rows, :], z)
            pre = dot(uvt[0, m], jnp.concatenate([msg, h.astype(BF16)], axis=0))
            result.append(add_silu(h, pre))
        return result

    def messages(m, h, part):
        rows = slice(m * C, (m + 1) * C)
        tiles = []
        for k in range(KB):
            for half in range(2):
                tiles.append(h[:, half * 128 : (half + 1) * 128] * fbc[k, rows, :])
        return dot(jnp.concatenate(tiles, axis=1), rad[part])

    for m, h in enumerate(first_layer(agg, hot_own)):
        rows = slice(m * C, (m + 1) * C)
        h_own[rows, :] = h
        acc[rows, :] = messages(m, h.astype(BF16), 0)

    wide_low = iota((32, 128), 1) < 64

    def agg_pair(first):
        return jnp.where(wide_low, agg_recv[first], agg_recv[first + 1])

    for c in agg_copies[0:3]:
        c.wait_recv()
    for m, h in enumerate(first_layer(jnp.concatenate([agg_pair(0), agg_recv[2]], axis=1), hot_early)):
        rows = slice(m * C, (m + 1) * C)
        acc[rows, :] += messages(m, h.astype(BF16), 1)
    for c in agg_copies[3:6]:
        c.wait_recv()
    message = []
    for m, h in enumerate(first_layer(jnp.concatenate([agg_recv[3], agg_pair(4)], axis=1), hot_late)):
        rows = slice(m * C, (m + 1) * C)
        message.append((acc[rows, :] + messages(m, h.astype(BF16), 2)).astype(BF16))

    forces = []
    loads[9].wait()
    for m in range(MODELS):
        rows = slice(m * C, (m + 1) * C)
        x = jnp.concatenate([message[m], h_own[rows, :].astype(BF16)], axis=0)
        h = add_silu(h_own[rows, :], dot(uvt[1, m], x))
        coeff = dot(fw_ref[m], h.astype(BF16))
        forces.append([SCALE * jnp.sum(coeff * dsum[c], axis=0, keepdims=True) for c in range(3)])
    loads[10].wait()
    alive = jnp.where(iota((1, ATOMS_DEV), 1) < live_ref[...], 1.0, 0.0)
    spread = jnp.zeros((1, ATOMS_DEV), F32)
    for c in range(3):
        mean = (forces[0][c] + forces[1][c] + forces[2][c] + forces[3][c]) * 0.25
        for m in range(MODELS):
            gap = forces[m][c] - mean
            spread = spread + gap * gap
        mean_ref[c : c + 1, :] = mean * alive
    dev_ref[...] = spread * 0.25 * alive

    for c in pack_copies + agg_copies:
        c.wait_send()


def solution(mesh):
    sizes = tuple(mesh.shape[a] for a in AXES)

    def local(positions, species, neighbors, atom_count, ghost_x, ghost_yz, embedding, filters, update_u, update_v, force_w):
        vmem = pl.BlockSpec(memory_space=pltpu.VMEM)
        anywhere = pl.BlockSpec(memory_space=pl.ANY)
        mean, spread = pl.pallas_call(
            functools.partial(kernel, sizes),
            out_shape=(pltpu.VMEM((3, ATOMS_DEV), F32), pltpu.VMEM((1, ATOMS_DEV), F32)),
            in_specs=[anywhere] * 11,
            out_specs=(vmem, vmem),
            scratch_shapes=[
                pltpu.VMEM((3, ATOMS_DEV), F32),
                pltpu.VMEM((1, ATOMS_DEV), jnp.int32),
                pltpu.VMEM((2 * SLOTS_HALF, ATOMS_DEV), jnp.int32),
                pltpu.VMEM((1, 1), jnp.int32),
                pltpu.VMEM((2, 128), jnp.int32),
                pltpu.VMEM((4, 64), jnp.int32),
                pltpu.VMEM((2, MODELS, C, C), BF16),
                pltpu.VMEM((2, MODELS, C, C), BF16),
                pltpu.VMEM((SPECIES, WIDTH), BF16),
                pltpu.VMEM((2, KB, WIDTH), BF16),
                pltpu.VMEM((MODELS, KB, C), BF16),
                pltpu.VMEM((ATOMS_DEV, GHOSTS), BF16),
                pltpu.VMEM((4, 8, 128), F32),
                pltpu.VMEM((6, 8, 128), F32),
                pltpu.VMEM((4, 32, 128), F32),
                pltpu.VMEM((6, 32, 128), F32),
                pltpu.VMEM((3 * SLOTS_HALF, 16, ATOMS_DEV), BF16),
                pltpu.VMEM((TABLE, ATOMS_DEV), BF16),
                pltpu.VMEM((TABLE, 8), F32),
                pltpu.VMEM((3, KB * 256, ATOMS_DEV), BF16),
                pltpu.VMEM((WIDTH, ATOMS_DEV), F32),
                pltpu.VMEM((WIDTH, KB * 256), BF16),
                pltpu.VMEM((WIDTH, ATOMS_DEV), F32),
                pltpu.VMEM((KB, WIDTH, 128), BF16),
                pltpu.VMEM((2, MODELS, C, 2 * C), BF16),
                pltpu.VMEM((WIDTH, 128), BF16),
                pltpu.VMEM((3, KB, ATOMS_DEV), F32),
                pltpu.VMEM((4, 32, ATOMS_DEV), F32),
                pltpu.SemaphoreType.DMA((12,)),
                pltpu.SemaphoreType.DMA((12,)),
                pltpu.SemaphoreType.DMA((11,)),
            ],
            compiler_params=pltpu.CompilerParams(
                collective_id=0, has_side_effects=True, vmem_limit_bytes=60 * 1024 * 1024
            ),
        )(
            positions,
            species.reshape(1, ATOMS_DEV),
            neighbors,
            atom_count.reshape(1, 1),
            ghost_x.reshape(2, 2 * 64),
            ghost_yz.reshape(4, 64),
            embedding,
            filters,
            update_u,
            update_v,
            jnp.swapaxes(force_w, 1, 2),
        )
        return mean, spread.reshape(ATOMS_DEV)

    split_spec = P(AXES)
    return jax.shard_map(
        local,
        mesh=mesh,
        in_specs=(
            P(None, AXES), split_spec, P(None, AXES), split_spec,
            P(AXES, None, None), P(AXES, None, None), P(), P(), P(), P(), P(),
        ),
        out_specs=(P(None, AXES), split_spec),
        check_vma=False,
    )
```

```python
import functools

import jax
import jax.numpy as jnp
from jax import lax
from jax.experimental import pallas as pl
from jax.experimental.pallas import tpu as pltpu
from jax.sharding import PartitionSpec as P

ATOMS_DEV = 256
GHOSTS = 512
TABLE = ATOMS_DEV + GHOSTS
MODELS = 4
C = 128
WIDTH = MODELS * C
KB = 8
SPECIES = 4
SLOTS_HALF = 32
SCALE = 0.125
ROOT_LOG2E = 1.2011224087864498
F32 = jnp.float32
BF16 = jnp.bfloat16
AXES = ("gx", "gy", "gz")


def iota(shape, dim):
    return lax.broadcasted_iota(jnp.int32, shape, dim)


def dot(a, b):
    return lax.dot_general(a, b, (((1,), (0,)), ((), ())), preferred_element_type=F32)


def split(x):
    high = x.astype(BF16).astype(F32)
    return high, (x - high).astype(BF16).astype(F32)


def add_silu(h, pre):
    half = 0.5 * pre
    return h + half + half * jnp.tanh(half)


LOG2E = 1.4426950408889634
DROP = 0.1353352832366127


def kernel(
    sizes,
    pos_hbm, spec_hbm, nbr_hbm, live_hbm, gx_hbm, gyz_hbm, emb_hbm, filt_hbm, u_hbm, v_hbm, fw_hbm,
    mean_ref, dev_ref,
    pos_ref, spec_ref, nbr_ref, live_ref, gx_ref, gyz_ref, u_vm, v_vm, emb_ref, filt_ref, fw_ref,
    sel, pack_send, pack_recv, agg_send, agg_recv, slots, count, col, rad_own, rad_pair, rad_z, rad_x, rad_y, h_own, h_tab, acc,
    fbc, uvt, w_msg, dsum, sent,
    send_sem, recv_sem, copy_sem,
):
    here = [lax.axis_index(a) for a in AXES]
    odd_x = lax.rem(here[0], 2)
    step_x = 1 - 2 * odd_x
    def peer(number, step):
        size = sizes[number]
        return {AXES[number]: lax.rem(here[number] + step + size, size)}

    peers = [peer(2, 1), peer(2, -1), peer(0, step_x), peer(0, -step_x), peer(1, 1), peer(1, -1)]

    barrier = pltpu.get_barrier_semaphore()
    for target in peers:
        pl.semaphore_signal(barrier, inc=1, device_id=target, device_id_type=pl.DeviceIdType.MESH)
    loads = [
        pltpu.make_async_copy(source, target, copy_sem.at[n])
        for n, (source, target) in enumerate(
            (
                (gx_hbm, gx_ref), (gyz_hbm, gyz_ref), (pos_hbm, pos_ref), (spec_hbm, spec_ref),
                (nbr_hbm, nbr_ref), (emb_hbm, emb_ref), (filt_hbm, filt_ref), (u_hbm, u_vm), (v_hbm, v_vm), (fw_hbm, fw_ref), (live_hbm, live_ref),
            )
        )
    ]
    for c in loads:
        c.start()
    for c in loads[0:4]:
        c.wait()

    lists = [
        jnp.concatenate([gyz_ref[2:3, :], gyz_ref[3:4, :]], axis=1),
        gx_ref[pl.ds(odd_x, 1), :],
        gx_ref[pl.ds(1 - odd_x, 1), :],
        jnp.concatenate([gyz_ref[0:1, :], gyz_ref[1:2, :]], axis=1),
    ]
    atom_row = iota((ATOMS_DEV, 128), 0)
    for g in range(4):
        sel[:, g * 128 : (g + 1) * 128] = jnp.where(atom_row == lists[g], 1.0, 0.0).astype(BF16)

    own = jnp.concatenate(
        [pos_ref[...], spec_ref[...].astype(F32), jnp.zeros((4, ATOMS_DEV), F32)], axis=0
    )
    high = own.astype(BF16).astype(F32)
    rest = own - high
    middle = rest.astype(BF16).astype(F32)
    low = rest - middle
    picked = dot(jnp.concatenate([high, middle, low], axis=0).astype(BF16), sel[...])
    picked = picked[0:8] + picked[8:16] + picked[16:24]
    for g in range(4):
        pack_send[g] = picked[:, g * 128 : (g + 1) * 128]

    def sends(source, target, first):
        return [
            pltpu.make_async_remote_copy(
                src_ref=source.at[group],
                dst_ref=target.at[face],
                send_sem=send_sem.at[first + face],
                recv_sem=recv_sem.at[first + face],
                device_id=peers[face],
                device_id_type=pl.DeviceIdType.MESH,
            )
            for face, group in enumerate((0, 0, 1, 2, 3, 3))
        ]

    pl.semaphore_wait(barrier, 6)
    pack_copies = sends(pack_send, pack_recv, 0)
    for n in (3, 4, 5, 0, 1, 2):
        pack_copies[n].start()

    loads[4].wait()
    for s in range(SLOTS_HALF):
        slots[s] = jnp.broadcast_to(nbr_ref[s : s + 1, :].astype(F32), (16, ATOMS_DEV)).astype(BF16)
        lent_id = jnp.broadcast_to(nbr_ref[SLOTS_HALF + s : SLOTS_HALF + s + 1, :].astype(F32), (16, ATOMS_DEV))
        slots[SLOTS_HALF + s] = (lent_id - 256.0).astype(BF16)
        slots[2 * SLOTS_HALF + s] = (lent_id - 512.0).astype(BF16)

    one = jnp.ones((16, ATOMS_DEV), BF16)
    nil = jnp.zeros((16, ATOMS_DEV), BF16)

    def count_rows(first_slot, base, first_row, rows):
        @pl.loop(0, rows // 64)
        def _(tile):
            which = [
                (iota((16, ATOMS_DEV), 0) + (tile * 64 + base + 16 * r)).astype(F32).astype(BF16)
                for r in range(4)
            ]
            total = [nil] * 4
            for s in range(first_slot, first_slot + SLOTS_HALF):
                ids = slots[s]
                total = [t + jnp.where(ids == w, one, nil) for t, w in zip(total, which)]
            for r in range(4):
                place = pl.ds(pl.multiple_of(tile * 64 + (first_row + 16 * r), 16), 16)
                count[place, :] = total[r]

    count_rows(0, 0, 0, 256)
    count_rows(2 * SLOTS_HALF, 128, 256, 128)
    count_rows(SLOTS_HALF, 128 * (1 - odd_x), 384, 128)
    count_rows(SLOTS_HALF, 128 * odd_x, 512, 128)
    count_rows(2 * SLOTS_HALF, 0, 640, 128)

    centre = own[0:3]

    def radial_rows(target, begin, many):
        rows = 32
        for tile in range(many // rows):
            first = begin + tile * rows
            squared = None
            for c in range(3):
                gap = col[first : first + rows, c : c + 1] - pos_ref[c : c + 1, :]
                squared = gap * gap if squared is None else squared + gap * gap
            off = squared * (2.0 * ROOT_LOG2E) - 4.0 * ROOT_LOG2E
            grow = squared * (4.0 * LOG2E)
            up = jnp.exp2(grow - 9.0 * LOG2E)
            down = jnp.exp2(7.0 * LOG2E - grow)
            mid = jnp.exp2(-(off * off)) * count[first : first + rows, :].astype(F32)

            def put(k, value):
                target[k * many + tile * rows : k * many + (tile + 1) * rows, :] = value.astype(BF16)

            put(4, mid)
            value = mid
            for k in (5, 6, 7):
                value = value * up
                put(k, value)
                up = up * DROP
            value = mid
            for k in (3, 2, 1, 0):
                value = value * down
                put(k, value)
                down = down * DROP

    def left_rows(packed):
        n = packed.shape[1]
        eight = iota((8, n), 0).astype(F32)
        hot = jnp.where(packed[3:4] == eight, 1.0, 0.0)
        hot_high = jnp.where(packed[3:4] == eight - 4.0, 1.0, 0.0)
        p_high, p_low = split(packed[0:3])
        place = jnp.concatenate([p_high, p_low, jnp.zeros((2, n), F32)], axis=0)
        blank = jnp.zeros((8, n), F32)
        even = jnp.concatenate([hot, place, blank, blank], axis=0)
        odd = jnp.concatenate([hot_high, blank, place, blank], axis=0)
        return jnp.concatenate([even.astype(BF16), odd.astype(BF16)], axis=1), hot

    def gather_sums(both, target):
        wide = target.shape[0] // 4
        return [dot(both, target[q * wide : (q + 1) * wide, :]) for q in range(4)]

    col[0:256, :] = own.T
    radial_rows(rad_own, 0, 256)
    both_own, hot_own = left_rows(own)
    for q, s in enumerate(gather_sums(both_own, rad_own)):
        sent[q] = s

    lane_low = iota((8, 128), 1) < 64
    sub = iota((8, 128), 0)

    def pair(first, axis):
        step = jnp.where(sub == axis, 1.0, 0.0)
        return jnp.where(lane_low, pack_recv[first] - step, pack_recv[first + 1] + step)

    near = jnp.where(sub == 0, step_x.astype(F32), 0.0)
    lent_hot = {}
    sums = [sent[q] for q in range(4)]
    for c in pack_copies[slice(2, 3)]:
        c.wait_recv()
    lent = pack_recv[2] + near
    col[384:512, :] = lent.T
    radial_rows(rad_pair, 384, 128)
    both_lent, lent_hot["p"] = left_rows(lent)
    sums = [a + b for a, b in zip(sums, gather_sums(both_lent, rad_pair))]

    for c in pack_copies[slice(0, 2)]:
        c.wait_recv()
    lent = pair(0, 2)
    col[256:384, :] = lent.T
    radial_rows(rad_z, 256, 128)
    both_lent, lent_hot["z"] = left_rows(lent)
    sums = [a + b for a, b in zip(sums, gather_sums(both_lent, rad_z))]

    for c in pack_copies[slice(3, 4)]:
        c.wait_recv()
    lent = pack_recv[3] - near
    col[512:640, :] = lent.T
    radial_rows(rad_x, 512, 128)
    both_lent, lent_hot["x"] = left_rows(lent)
    sums = [a + b for a, b in zip(sums, gather_sums(both_lent, rad_x))]

    for c in pack_copies[slice(4, 6)]:
        c.wait_recv()
    lent = pair(4, 1)
    col[640:768, :] = lent.T
    radial_rows(rad_y, 640, 128)
    both_lent, lent_hot["y"] = left_rows(lent)
    sums = [a + b for a, b in zip(sums, gather_sums(both_lent, rad_y))]

    agg = jnp.concatenate([s[0:8] for s in sums], axis=0)
    a_high, a_low = split(agg)
    chosen = dot(jnp.concatenate([a_high, a_low], axis=0).astype(BF16), sel[...])
    chosen = chosen[0:32] + chosen[32:64]
    for g in range(4):
        agg_send[g] = chosen[:, g * 128 : (g + 1) * 128]
    agg_copies = sends(agg_send, agg_recv, 6)
    for n in (3, 4, 5, 0, 1, 2):
        agg_copies[n].start()

    loads[5].wait()
    loads[6].wait()
    filt = filt_ref[...].astype(F32)
    emb = emb_ref[...].astype(F32)
    emb8 = jnp.concatenate([emb, emb], axis=0)
    upper = iota((8, WIDTH), 0) < 4
    first_w = jnp.concatenate(
        [
            SCALE * emb8 * jnp.where(upper, filt[0, 2 * q : 2 * q + 1], filt[0, 2 * q + 1 : 2 * q + 2])
            for q in range(4)
        ],
        axis=0,
    )
    w_high, w_low = split(first_w)
    w_msg[...] = jnp.concatenate([w_high, w_high, w_low, jnp.where(upper, emb8, 0.0), SCALE * filt[1], jnp.zeros((16, WIDTH), F32)], axis=0).T.astype(BF16)
    for k in range(KB):
        ones = jnp.where(iota((128, 128), 0) == 104 + k, 1.0, 0.0).astype(BF16)
        fbc[k] = dot(w_msg[...], ones).astype(BF16)
    loads[7].wait()
    loads[8].wait()
    for l in range(2):
        for m in range(MODELS):
            uvt[l, m, :, 0:128] = u_vm[l, m].astype(F32).T.astype(BF16)
            uvt[l, m, :, 128:256] = v_vm[l, m].astype(F32).T.astype(BF16)

    for q in range(4):
        for odd in range(2):
            k = 2 * q + odd
            weight = jnp.sum(sums[q][4 * odd : 4 * odd + 4], axis=0, keepdims=True)
            base = 8 + 8 * odd
            for c in range(3):
                dsum[c, k : k + 1, :] = (
                    sums[q][base + c : base + c + 1]
                    + sums[q][base + 3 + c : base + 4 + c]
                    - centre[c : c + 1] * weight
                )

    def first_layer(table, hot):
        n = table.shape[1]
        t_high, t_low = split(table)
        blank = jnp.zeros((32, n), F32)
        x = jnp.concatenate([t_high, t_low, t_high, blank], axis=0).astype(BF16)
        z = jnp.concatenate([blank, blank, blank, hot, blank[0:24]], axis=0).astype(BF16)
        result = []
        for m in range(MODELS):
            rows = slice(m * C, (m + 1) * C)
            msg = dot(w_msg[rows, :], x).astype(BF16)
            h = dot(w_msg[rows, :], z)
            pre = dot(uvt[0, m], jnp.concatenate([msg, h.astype(BF16)], axis=0))
            result.append(add_silu(h, pre))
        return result

    def messages(m, h, part):
        rows = slice(m * C, (m + 1) * C)
        tiles = []
        for k in range(KB):
            for half in range(h.shape[1] // 128):
                tiles.append(h[:, half * 128 : (half + 1) * 128] * fbc[k, rows, :])
        return dot(jnp.concatenate(tiles, axis=1), part[...])

    for m, h in enumerate(first_layer(agg, hot_own)):
        rows = slice(m * C, (m + 1) * C)
        h_own[rows, :] = h
        acc[rows, :] = messages(m, h.astype(BF16), rad_own)

    wide_low = iota((32, 128), 1) < 64

    def agg_pair(first):
        return jnp.where(wide_low, agg_recv[first], agg_recv[first + 1])

    for c in agg_copies[slice(2, 3)]:
        c.wait_recv()
    for m, h in enumerate(first_layer(agg_recv[2], lent_hot["p"])):
        rows = slice(m * C, (m + 1) * C)
        acc[rows, :] += messages(m, h.astype(BF16), rad_pair)
    for c in agg_copies[slice(0, 2)]:
        c.wait_recv()
    for m, h in enumerate(first_layer(agg_pair(0), lent_hot["z"])):
        rows = slice(m * C, (m + 1) * C)
        acc[rows, :] += messages(m, h.astype(BF16), rad_z)
    for c in agg_copies[slice(3, 4)]:
        c.wait_recv()
    for m, h in enumerate(first_layer(agg_recv[3], lent_hot["x"])):
        rows = slice(m * C, (m + 1) * C)
        acc[rows, :] += messages(m, h.astype(BF16), rad_x)
    for c in agg_copies[slice(4, 6)]:
        c.wait_recv()
    message = []
    for m, h in enumerate(first_layer(agg_pair(4), lent_hot["y"])):
        rows = slice(m * C, (m + 1) * C)
        message.append((acc[rows, :] + messages(m, h.astype(BF16), rad_y)).astype(BF16))

    forces = []
    loads[9].wait()
    for m in range(MODELS):
        rows = slice(m * C, (m + 1) * C)
        x = jnp.concatenate([message[m], h_own[rows, :].astype(BF16)], axis=0)
        h = add_silu(h_own[rows, :], dot(uvt[1, m], x))
        coeff = dot(fw_ref[m], h.astype(BF16))
        forces.append([SCALE * jnp.sum(coeff * dsum[c], axis=0, keepdims=True) for c in range(3)])
    loads[10].wait()
    alive = jnp.where(iota((1, ATOMS_DEV), 1) < live_ref[...], 1.0, 0.0)
    spread = jnp.zeros((1, ATOMS_DEV), F32)
    for c in range(3):
        mean = (forces[0][c] + forces[1][c] + forces[2][c] + forces[3][c]) * 0.25
        for m in range(MODELS):
            gap = forces[m][c] - mean
            spread = spread + gap * gap
        mean_ref[c : c + 1, :] = mean * alive
    dev_ref[...] = spread * 0.25 * alive

    for c in pack_copies + agg_copies:
        c.wait_send()


def solution(mesh):
    sizes = tuple(mesh.shape[a] for a in AXES)

    def local(positions, species, neighbors, atom_count, ghost_x, ghost_yz, embedding, filters, update_u, update_v, force_w):
        vmem = pl.BlockSpec(memory_space=pltpu.VMEM)
        anywhere = pl.BlockSpec(memory_space=pl.ANY)
        mean, spread = pl.pallas_call(
            functools.partial(kernel, sizes),
            out_shape=(pltpu.VMEM((3, ATOMS_DEV), F32), pltpu.VMEM((1, ATOMS_DEV), F32)),
            in_specs=[anywhere] * 11,
            out_specs=(vmem, vmem),
            scratch_shapes=[
                pltpu.VMEM((3, ATOMS_DEV), F32),
                pltpu.VMEM((1, ATOMS_DEV), jnp.int32),
                pltpu.VMEM((2 * SLOTS_HALF, ATOMS_DEV), jnp.int32),
                pltpu.VMEM((1, 1), jnp.int32),
                pltpu.VMEM((2, 128), jnp.int32),
                pltpu.VMEM((4, 64), jnp.int32),
                pltpu.VMEM((2, MODELS, C, C), BF16),
                pltpu.VMEM((2, MODELS, C, C), BF16),
                pltpu.VMEM((SPECIES, WIDTH), BF16),
                pltpu.VMEM((2, KB, WIDTH), BF16),
                pltpu.VMEM((MODELS, KB, C), BF16),
                pltpu.VMEM((ATOMS_DEV, GHOSTS), BF16),
                pltpu.VMEM((4, 8, 128), F32),
                pltpu.VMEM((6, 8, 128), F32),
                pltpu.VMEM((4, 32, 128), F32),
                pltpu.VMEM((6, 32, 128), F32),
                pltpu.VMEM((3 * SLOTS_HALF, 16, ATOMS_DEV), BF16),
                pltpu.VMEM((TABLE, ATOMS_DEV), BF16),
                pltpu.VMEM((TABLE, 8), F32),
                pltpu.VMEM((KB * 256, ATOMS_DEV), BF16),
                pltpu.VMEM((KB * 128, ATOMS_DEV), BF16),
                pltpu.VMEM((KB * 128, ATOMS_DEV), BF16),
                pltpu.VMEM((KB * 128, ATOMS_DEV), BF16),
                pltpu.VMEM((KB * 128, ATOMS_DEV), BF16),
                pltpu.VMEM((WIDTH, ATOMS_DEV), F32),
                pltpu.VMEM((WIDTH, KB * 256), BF16),
                pltpu.VMEM((WIDTH, ATOMS_DEV), F32),
                pltpu.VMEM((KB, WIDTH, 128), BF16),
                pltpu.VMEM((2, MODELS, C, 2 * C), BF16),
                pltpu.VMEM((WIDTH, 128), BF16),
                pltpu.VMEM((3, KB, ATOMS_DEV), F32),
                pltpu.VMEM((4, 32, ATOMS_DEV), F32),
                pltpu.SemaphoreType.DMA((12,)),
                pltpu.SemaphoreType.DMA((12,)),
                pltpu.SemaphoreType.DMA((11,)),
            ],
            compiler_params=pltpu.CompilerParams(
                collective_id=0, has_side_effects=True, vmem_limit_bytes=60 * 1024 * 1024
            ),
        )(
            positions,
            species.reshape(1, ATOMS_DEV),
            neighbors,
            atom_count.reshape(1, 1),
            ghost_x.reshape(2, 2 * 64),
            ghost_yz.reshape(4, 64),
            embedding,
            filters,
            update_u,
            update_v,
            jnp.swapaxes(force_w, 1, 2),
        )
        return mean, spread.reshape(ATOMS_DEV)

    split_spec = P(AXES)
    return jax.shard_map(
        local,
        mesh=mesh,
        in_specs=(
            P(None, AXES), split_spec, P(None, AXES), split_spec,
            P(AXES, None, None), P(AXES, None, None), P(), P(), P(), P(), P(),
        ),
        out_specs=(P(None, AXES), split_spec),
        check_vma=False,
    )
```

```python
import functools

import jax
import jax.numpy as jnp
from jax import lax
from jax.experimental import pallas as pl
from jax.experimental.pallas import tpu as pltpu
from jax.sharding import PartitionSpec as P

ATOMS_DEV = 256
GHOSTS = 512
TABLE = ATOMS_DEV + GHOSTS
MODELS = 4
C = 128
WIDTH = MODELS * C
KB = 8
SPECIES = 4
SLOTS_HALF = 32
SCALE = 0.125
ROOT_LOG2E = 1.2011224087864498
F32 = jnp.float32
BF16 = jnp.bfloat16
AXES = ("gx", "gy", "gz")


def iota(shape, dim):
    return lax.broadcasted_iota(jnp.int32, shape, dim)


def dot(a, b):
    return lax.dot_general(a, b, (((1,), (0,)), ((), ())), preferred_element_type=F32)


def split(x):
    high = x.astype(BF16).astype(F32)
    return high, (x - high).astype(BF16).astype(F32)


def add_silu(h, pre):
    half = 0.5 * pre
    return h + half + half * jnp.tanh(half)


LOG2E = 1.4426950408889634
DROP = 0.1353352832366127


def kernel(
    sizes,
    pos_hbm, spec_hbm, nbr_hbm, live_hbm, gx_hbm, gyz_hbm, emb_hbm, filt_hbm, u_hbm, v_hbm, fw_hbm,
    mean_ref, dev_ref,
    pos_ref, spec_ref, nbr_ref, live_ref, gx_ref, gyz_ref, u_vm, v_vm, emb_ref, filt_ref, fw_ref,
    sel, pack_send, pack_recv, agg_send, agg_recv, slots, count, col, rad_own, rad_pair, rad_z, rad_x, rad_y, h_own, h_tab, acc,
    fbc, uvt, w_msg, dsum, sent,
    send_sem, recv_sem, copy_sem,
):
    here = [lax.axis_index(a) for a in AXES]
    odd_x = lax.rem(here[0], 2)
    step_x = 1 - 2 * odd_x
    def peer(number, step):
        size = sizes[number]
        return {AXES[number]: lax.rem(here[number] + step + size, size)}

    peers = [peer(2, 1), peer(2, -1), peer(0, step_x), peer(0, -step_x), peer(1, 1), peer(1, -1)]

    barrier = pltpu.get_barrier_semaphore()
    for target in peers:
        pl.semaphore_signal(barrier, inc=1, device_id=target, device_id_type=pl.DeviceIdType.MESH)
    loads = [
        pltpu.make_async_copy(source, target, copy_sem.at[n])
        for n, (source, target) in enumerate(
            (
                (gx_hbm, gx_ref), (gyz_hbm, gyz_ref), (pos_hbm, pos_ref), (spec_hbm, spec_ref),
                (nbr_hbm, nbr_ref), (emb_hbm, emb_ref), (filt_hbm, filt_ref), (u_hbm, u_vm), (v_hbm, v_vm), (fw_hbm, fw_ref), (live_hbm, live_ref),
            )
        )
    ]
    for c in loads:
        c.start()
    for c in loads[0:4]:
        c.wait()

    lists = [
        jnp.concatenate([gyz_ref[2:3, :], gyz_ref[3:4, :]], axis=1),
        gx_ref[pl.ds(odd_x, 1), :],
        gx_ref[pl.ds(1 - odd_x, 1), :],
        jnp.concatenate([gyz_ref[0:1, :], gyz_ref[1:2, :]], axis=1),
    ]
    atom_row = iota((ATOMS_DEV, 128), 0)
    for g in range(4):
        sel[:, g * 128 : (g + 1) * 128] = jnp.where(atom_row == lists[g], 1.0, 0.0).astype(BF16)

    own = jnp.concatenate(
        [pos_ref[...], spec_ref[...].astype(F32), jnp.zeros((4, ATOMS_DEV), F32)], axis=0
    )
    high = own.astype(BF16).astype(F32)
    rest = own - high
    middle = rest.astype(BF16).astype(F32)
    low = rest - middle
    picked = dot(jnp.concatenate([high, middle, low], axis=0).astype(BF16), sel[...])
    picked = picked[0:8] + picked[8:16] + picked[16:24]
    for g in range(4):
        pack_send[g] = picked[:, g * 128 : (g + 1) * 128]

    def sends(source, target, first):
        return [
            pltpu.make_async_remote_copy(
                src_ref=source.at[group],
                dst_ref=target.at[face],
                send_sem=send_sem.at[first + face],
                recv_sem=recv_sem.at[first + face],
                device_id=peers[face],
                device_id_type=pl.DeviceIdType.MESH,
            )
            for face, group in enumerate((0, 0, 1, 2, 3, 3))
        ]

    pl.semaphore_wait(barrier, 6)
    pack_copies = sends(pack_send, pack_recv, 0)
    for n in (3, 4, 5, 0, 1, 2):
        pack_copies[n].start()

    loads[4].wait()
    for s in range(SLOTS_HALF):
        slots[s] = jnp.broadcast_to(nbr_ref[s : s + 1, :].astype(F32), (16, ATOMS_DEV)).astype(BF16)
        lent_id = jnp.broadcast_to(nbr_ref[SLOTS_HALF + s : SLOTS_HALF + s + 1, :].astype(F32), (16, ATOMS_DEV))
        slots[SLOTS_HALF + s] = (lent_id - 256.0).astype(BF16)
        slots[2 * SLOTS_HALF + s] = (lent_id - 512.0).astype(BF16)

    one = jnp.ones((16, ATOMS_DEV), BF16)
    nil = jnp.zeros((16, ATOMS_DEV), BF16)

    def count_rows(first_slot, base, first_row, rows):
        @pl.loop(0, rows // 64)
        def _(tile):
            which = [
                (iota((16, ATOMS_DEV), 0) + (tile * 64 + base + 16 * r)).astype(F32).astype(BF16)
                for r in range(4)
            ]
            total = [nil] * 4
            for s in range(first_slot, first_slot + SLOTS_HALF):
                ids = slots[s]
                total = [t + jnp.where(ids == w, one, nil) for t, w in zip(total, which)]
            for r in range(4):
                place = pl.ds(pl.multiple_of(tile * 64 + (first_row + 16 * r), 16), 16)
                count[place, :] = total[r]

    count_rows(0, 0, 0, 256)
    count_rows(2 * SLOTS_HALF, 128, 256, 128)
    count_rows(SLOTS_HALF, 128 * (1 - odd_x), 384, 128)
    count_rows(SLOTS_HALF, 128 * odd_x, 512, 128)
    count_rows(2 * SLOTS_HALF, 0, 640, 128)

    centre = own[0:3]

    def radial_rows(target, begin, many):
        rows = 32
        for tile in range(many // rows):
            first = begin + tile * rows
            squared = None
            for c in range(3):
                gap = col[first : first + rows, c : c + 1] - pos_ref[c : c + 1, :]
                squared = gap * gap if squared is None else squared + gap * gap
            off = squared * (2.0 * ROOT_LOG2E) - 4.0 * ROOT_LOG2E
            grow = squared * (4.0 * LOG2E)
            up = jnp.exp2(grow - 9.0 * LOG2E)
            down = jnp.exp2(7.0 * LOG2E - grow)
            mid = jnp.exp2(-(off * off)) * count[first : first + rows, :].astype(F32)

            def put(k, value):
                target[k * many + tile * rows : k * many + (tile + 1) * rows, :] = value.astype(BF16)

            put(4, mid)
            value = mid
            for k in (5, 6, 7):
                value = value * up
                put(k, value)
                up = up * DROP
            value = mid
            for k in (3, 2, 1, 0):
                value = value * down
                put(k, value)
                down = down * DROP

    def left_rows(packed):
        n = packed.shape[1]
        eight = iota((8, n), 0).astype(F32)
        hot = jnp.where(packed[3:4] == eight, 1.0, 0.0)
        hot_high = jnp.where(packed[3:4] == eight - 4.0, 1.0, 0.0)
        p_high, p_low = split(packed[0:3])
        place = jnp.concatenate([p_high, p_low, jnp.zeros((2, n), F32)], axis=0)
        blank = jnp.zeros((8, n), F32)
        even = jnp.concatenate([hot, place, blank, blank], axis=0)
        odd = jnp.concatenate([hot_high, blank, place, blank], axis=0)
        return jnp.concatenate([even.astype(BF16), odd.astype(BF16)], axis=1), hot

    def gather_sums(both, target):
        wide = target.shape[0] // 4
        return [dot(both, target[q * wide : (q + 1) * wide, :]) for q in range(4)]

    col[0:256, :] = own.T
    radial_rows(rad_own, 0, 256)
    both_own, hot_own = left_rows(own)
    for q, s in enumerate(gather_sums(both_own, rad_own)):
        sent[q] = s

    loads[5].wait()
    loads[6].wait()
    filt = filt_ref[...].astype(F32)
    emb = emb_ref[...].astype(F32)
    emb8 = jnp.concatenate([emb, emb], axis=0)
    upper = iota((8, WIDTH), 0) < 4
    first_w = jnp.concatenate(
        [
            SCALE * emb8 * jnp.where(upper, filt[0, 2 * q : 2 * q + 1], filt[0, 2 * q + 1 : 2 * q + 2])
            for q in range(4)
        ],
        axis=0,
    )
    w_high, w_low = split(first_w)
    w_msg[...] = jnp.concatenate([w_high, w_high, w_low, jnp.where(upper, emb8, 0.0), SCALE * filt[1], jnp.zeros((16, WIDTH), F32)], axis=0).T.astype(BF16)
    for k in range(KB):
        ones = jnp.where(iota((128, 128), 0) == 104 + k, 1.0, 0.0).astype(BF16)
        fbc[k] = dot(w_msg[...], ones).astype(BF16)
    lane_low = iota((8, 128), 1) < 64
    sub = iota((8, 128), 0)

    def pair(first, axis):
        step = jnp.where(sub == axis, 1.0, 0.0)
        return jnp.where(lane_low, pack_recv[first] - step, pack_recv[first + 1] + step)

    near = jnp.where(sub == 0, step_x.astype(F32), 0.0)
    lent_hot = {}
    sums = [sent[q] for q in range(4)]
    for c in pack_copies[slice(2, 3)]:
        c.wait_recv()
    lent = pack_recv[2] + near
    col[384:512, :] = lent.T
    radial_rows(rad_pair, 384, 128)
    both_lent, lent_hot["p"] = left_rows(lent)
    sums = [a + b for a, b in zip(sums, gather_sums(both_lent, rad_pair))]

    for c in pack_copies[slice(0, 2)]:
        c.wait_recv()
    lent = pair(0, 2)
    col[256:384, :] = lent.T
    radial_rows(rad_z, 256, 128)
    both_lent, lent_hot["z"] = left_rows(lent)
    sums = [a + b for a, b in zip(sums, gather_sums(both_lent, rad_z))]

    for c in pack_copies[slice(3, 4)]:
        c.wait_recv()
    lent = pack_recv[3] - near
    col[512:640, :] = lent.T
    radial_rows(rad_x, 512, 128)
    both_lent, lent_hot["x"] = left_rows(lent)
    sums = [a + b for a, b in zip(sums, gather_sums(both_lent, rad_x))]

    for c in pack_copies[slice(4, 6)]:
        c.wait_recv()
    lent = pair(4, 1)
    col[640:768, :] = lent.T
    radial_rows(rad_y, 640, 128)
    both_lent, lent_hot["y"] = left_rows(lent)
    sums = [a + b for a, b in zip(sums, gather_sums(both_lent, rad_y))]

    agg = jnp.concatenate([s[0:8] for s in sums], axis=0)
    a_high, a_low = split(agg)
    chosen = dot(jnp.concatenate([a_high, a_low], axis=0).astype(BF16), sel[...])
    chosen = chosen[0:32] + chosen[32:64]
    for g in range(4):
        agg_send[g] = chosen[:, g * 128 : (g + 1) * 128]
    agg_copies = sends(agg_send, agg_recv, 6)
    for n in (3, 4, 5, 0, 1, 2):
        agg_copies[n].start()

    loads[7].wait()
    loads[8].wait()
    for l in range(2):
        for m in range(MODELS):
            uvt[l, m, :, 0:128] = u_vm[l, m].astype(F32).T.astype(BF16)
            uvt[l, m, :, 128:256] = v_vm[l, m].astype(F32).T.astype(BF16)

    for q in range(4):
        for odd in range(2):
            k = 2 * q + odd
            weight = jnp.sum(sums[q][4 * odd : 4 * odd + 4], axis=0, keepdims=True)
            base = 8 + 8 * odd
            for c in range(3):
                dsum[c, k : k + 1, :] = (
                    sums[q][base + c : base + c + 1]
                    + sums[q][base + 3 + c : base + 4 + c]
                    - centre[c : c + 1] * weight
                )

    def first_layer(table, hot):
        n = table.shape[1]
        t_high, t_low = split(table)
        blank = jnp.zeros((32, n), F32)
        x = jnp.concatenate([t_high, t_low, t_high, blank], axis=0).astype(BF16)
        z = jnp.concatenate([blank, blank, blank, hot, blank[0:24]], axis=0).astype(BF16)
        result = []
        for m in range(MODELS):
            rows = slice(m * C, (m + 1) * C)
            msg = dot(w_msg[rows, :], x).astype(BF16)
            h = dot(w_msg[rows, :], z)
            pre = dot(uvt[0, m], jnp.concatenate([msg, h.astype(BF16)], axis=0))
            result.append(add_silu(h, pre))
        return result

    def messages(m, h, part):
        rows = slice(m * C, (m + 1) * C)
        tiles = []
        for k in range(KB):
            for half in range(h.shape[1] // 128):
                tiles.append(h[:, half * 128 : (half + 1) * 128] * fbc[k, rows, :])
        return dot(jnp.concatenate(tiles, axis=1), part[...])

    for m, h in enumerate(first_layer(agg, hot_own)):
        rows = slice(m * C, (m + 1) * C)
        h_own[rows, :] = h
        acc[rows, :] = messages(m, h.astype(BF16), rad_own)

    wide_low = iota((32, 128), 1) < 64

    def agg_pair(first):
        return jnp.where(wide_low, agg_recv[first], agg_recv[first + 1])

    for c in agg_copies[slice(2, 3)]:
        c.wait_recv()
    for m, h in enumerate(first_layer(agg_recv[2], lent_hot["p"])):
        rows = slice(m * C, (m + 1) * C)
        acc[rows, :] += messages(m, h.astype(BF16), rad_pair)
    for c in agg_copies[slice(0, 2)]:
        c.wait_recv()
    for m, h in enumerate(first_layer(agg_pair(0), lent_hot["z"])):
        rows = slice(m * C, (m + 1) * C)
        acc[rows, :] += messages(m, h.astype(BF16), rad_z)
    for c in agg_copies[slice(3, 4)]:
        c.wait_recv()
    for m, h in enumerate(first_layer(agg_recv[3], lent_hot["x"])):
        rows = slice(m * C, (m + 1) * C)
        acc[rows, :] += messages(m, h.astype(BF16), rad_x)
    for c in agg_copies[slice(4, 6)]:
        c.wait_recv()
    message = []
    for m, h in enumerate(first_layer(agg_pair(4), lent_hot["y"])):
        rows = slice(m * C, (m + 1) * C)
        message.append((acc[rows, :] + messages(m, h.astype(BF16), rad_y)).astype(BF16))

    forces = []
    loads[9].wait()
    for m in range(MODELS):
        rows = slice(m * C, (m + 1) * C)
        x = jnp.concatenate([message[m], h_own[rows, :].astype(BF16)], axis=0)
        h = add_silu(h_own[rows, :], dot(uvt[1, m], x))
        coeff = dot(fw_ref[m], h.astype(BF16))
        forces.append([SCALE * jnp.sum(coeff * dsum[c], axis=0, keepdims=True) for c in range(3)])
    loads[10].wait()
    alive = jnp.where(iota((1, ATOMS_DEV), 1) < live_ref[0], 1.0, 0.0)
    spread = jnp.zeros((1, ATOMS_DEV), F32)
    for c in range(3):
        mean = (forces[0][c] + forces[1][c] + forces[2][c] + forces[3][c]) * 0.25
        for m in range(MODELS):
            gap = forces[m][c] - mean
            spread = spread + gap * gap
        mean_ref[c : c + 1, :] = mean * alive
    dev_ref[...] = spread * 0.25 * alive

    for c in pack_copies + agg_copies:
        c.wait_send()


def solution(mesh):
    sizes = tuple(mesh.shape[a] for a in AXES)

    def local(positions, species, neighbors, atom_count, ghost_x, ghost_yz, embedding, filters, update_u, update_v, force_w):
        vmem = pl.BlockSpec(memory_space=pltpu.VMEM)
        anywhere = pl.BlockSpec(memory_space=pl.ANY)
        mean, spread = pl.pallas_call(
            functools.partial(kernel, sizes),
            out_shape=(pltpu.VMEM((3, ATOMS_DEV), F32), pltpu.VMEM((1, ATOMS_DEV), F32)),
            in_specs=[anywhere] * 11,
            out_specs=(vmem, vmem),
            scratch_shapes=[
                pltpu.VMEM((3, ATOMS_DEV), F32),
                pltpu.VMEM((1, ATOMS_DEV), jnp.int32),
                pltpu.VMEM((2 * SLOTS_HALF, ATOMS_DEV), jnp.int32),
                pltpu.SMEM((1,), jnp.int32),
                pltpu.VMEM((2, 128), jnp.int32),
                pltpu.VMEM((4, 64), jnp.int32),
                pltpu.VMEM((2, MODELS, C, C), BF16),
                pltpu.VMEM((2, MODELS, C, C), BF16),
                pltpu.VMEM((SPECIES, WIDTH), BF16),
                pltpu.VMEM((2, KB, WIDTH), BF16),
                pltpu.VMEM((MODELS, KB, C), BF16),
                pltpu.VMEM((ATOMS_DEV, GHOSTS), BF16),
                pltpu.VMEM((4, 8, 128), F32),
                pltpu.VMEM((6, 8, 128), F32),
                pltpu.VMEM((4, 32, 128), F32),
                pltpu.VMEM((6, 32, 128), F32),
                pltpu.VMEM((3 * SLOTS_HALF, 16, ATOMS_DEV), BF16),
                pltpu.VMEM((TABLE, ATOMS_DEV), BF16),
                pltpu.VMEM((TABLE, 8), F32),
                pltpu.VMEM((KB * 256, ATOMS_DEV), BF16),
                pltpu.VMEM((KB * 128, ATOMS_DEV), BF16),
                pltpu.VMEM((KB * 128, ATOMS_DEV), BF16),
                pltpu.VMEM((KB * 128, ATOMS_DEV), BF16),
                pltpu.VMEM((KB * 128, ATOMS_DEV), BF16),
                pltpu.VMEM((WIDTH, ATOMS_DEV), F32),
                pltpu.VMEM((WIDTH, KB * 256), BF16),
                pltpu.VMEM((WIDTH, ATOMS_DEV), F32),
                pltpu.VMEM((KB, WIDTH, 128), BF16),
                pltpu.VMEM((2, MODELS, C, 2 * C), BF16),
                pltpu.VMEM((WIDTH, 128), BF16),
                pltpu.VMEM((3, KB, ATOMS_DEV), F32),
                pltpu.VMEM((4, 32, ATOMS_DEV), F32),
                pltpu.SemaphoreType.DMA((12,)),
                pltpu.SemaphoreType.DMA((12,)),
                pltpu.SemaphoreType.DMA((11,)),
            ],
            compiler_params=pltpu.CompilerParams(
                collective_id=0, has_side_effects=True, vmem_limit_bytes=60 * 1024 * 1024
            ),
        )(
            positions,
            species.reshape(1, ATOMS_DEV),
            neighbors,
            atom_count,
            ghost_x.reshape(2, 2 * 64),
            ghost_yz.reshape(4, 64),
            embedding,
            filters,
            update_u,
            update_v,
            jnp.swapaxes(force_w, 1, 2),
        )
        return mean, spread.reshape(ATOMS_DEV)

    split_spec = P(AXES)
    return jax.shard_map(
        local,
        mesh=mesh,
        in_specs=(
            P(None, AXES), split_spec, P(None, AXES), split_spec,
            P(AXES, None, None), P(AXES, None, None), P(), P(), P(), P(), P(),
        ),
        out_specs=(P(None, AXES), split_spec),
        check_vma=False,
    )
```

```python
import functools

import jax
import jax.numpy as jnp
from jax import lax
from jax.experimental import pallas as pl
from jax.experimental.pallas import tpu as pltpu
from jax.sharding import PartitionSpec as P

ATOMS_DEV = 256
GHOSTS = 512
TABLE = ATOMS_DEV + GHOSTS
MODELS = 4
C = 128
WIDTH = MODELS * C
KB = 8
SPECIES = 4
SLOTS_HALF = 32
SCALE = 0.125
ROOT_LOG2E = 1.2011224087864498
F32 = jnp.float32
BF16 = jnp.bfloat16
AXES = ("gx", "gy", "gz")


def iota(shape, dim):
    return lax.broadcasted_iota(jnp.int32, shape, dim)


def dot(a, b):
    return lax.dot_general(a, b, (((1,), (0,)), ((), ())), preferred_element_type=F32)


def split(x):
    high = x.astype(BF16).astype(F32)
    return high, (x - high).astype(BF16).astype(F32)


def add_silu(h, pre):
    half = 0.5 * pre
    return h + half + half * jnp.tanh(half)


LOG2E = 1.4426950408889634
DROP = 0.1353352832366127


def kernel(
    sizes,
    pos_hbm, spec_hbm, nbr_hbm, live_hbm, gx_hbm, gyz_hbm, emb_ref, filt_ref, u_hbm, v_hbm, fw_ref,
    mean_ref, dev_ref,
    pos_ref, spec_ref, nbr_ref, live_ref, gx_ref, gyz_ref, u_vm, v_vm,
    sel, pack_send, pack_recv, agg_send, agg_recv, slots, count, col, rad_own, rad_pair, rad_z, rad_x, rad_y, h_own, h_tab, acc,
    fbc, uvt, w_msg, dsum, sent,
    send_sem, recv_sem, copy_sem,
):
    here = [lax.axis_index(a) for a in AXES]
    odd_x = lax.rem(here[0], 2)
    step_x = 1 - 2 * odd_x
    def peer(number, step):
        size = sizes[number]
        return {AXES[number]: lax.rem(here[number] + step + size, size)}

    peers = [peer(2, 1), peer(2, -1), peer(0, step_x), peer(0, -step_x), peer(1, 1), peer(1, -1)]

    barrier = pltpu.get_barrier_semaphore()
    for target in peers:
        pl.semaphore_signal(barrier, inc=1, device_id=target, device_id_type=pl.DeviceIdType.MESH)
    loads = [
        pltpu.make_async_copy(source, target, copy_sem.at[n])
        for n, (source, target) in enumerate(
            (
                (gx_hbm, gx_ref), (gyz_hbm, gyz_ref), (pos_hbm, pos_ref), (spec_hbm, spec_ref),
                (nbr_hbm, nbr_ref), (u_hbm, u_vm), (v_hbm, v_vm), (live_hbm, live_ref),
            )
        )
    ]
    for c in loads:
        c.start()
    for c in loads[0:4]:
        c.wait()

    lists = [
        jnp.concatenate([gyz_ref[2:3, :], gyz_ref[3:4, :]], axis=1),
        gx_ref[pl.ds(odd_x, 1), :],
        gx_ref[pl.ds(1 - odd_x, 1), :],
        jnp.concatenate([gyz_ref[0:1, :], gyz_ref[1:2, :]], axis=1),
    ]
    atom_row = iota((ATOMS_DEV, 128), 0)
    for g in range(4):
        sel[:, g * 128 : (g + 1) * 128] = jnp.where(atom_row == lists[g], 1.0, 0.0).astype(BF16)

    own = jnp.concatenate(
        [pos_ref[...], spec_ref[...].astype(F32), jnp.zeros((4, ATOMS_DEV), F32)], axis=0
    )
    high = own.astype(BF16).astype(F32)
    rest = own - high
    middle = rest.astype(BF16).astype(F32)
    low = rest - middle
    picked = dot(jnp.concatenate([high, middle, low], axis=0).astype(BF16), sel[...])
    picked = picked[0:8] + picked[8:16] + picked[16:24]
    for g in range(4):
        pack_send[g] = picked[:, g * 128 : (g + 1) * 128]

    def sends(source, target, first):
        return [
            pltpu.make_async_remote_copy(
                src_ref=source.at[group],
                dst_ref=target.at[face],
                send_sem=send_sem.at[first + face],
                recv_sem=recv_sem.at[first + face],
                device_id=peers[face],
                device_id_type=pl.DeviceIdType.MESH,
            )
            for face, group in enumerate((0, 0, 1, 2, 3, 3))
        ]

    pl.semaphore_wait(barrier, 6)
    pack_copies = sends(pack_send, pack_recv, 0)
    for n in (3, 4, 5, 0, 1, 2):
        pack_copies[n].start()

    loads[4].wait()
    for s in range(SLOTS_HALF):
        slots[s] = jnp.broadcast_to(nbr_ref[s : s + 1, :].astype(F32), (16, ATOMS_DEV)).astype(BF16)
        lent_id = jnp.broadcast_to(nbr_ref[SLOTS_HALF + s : SLOTS_HALF + s + 1, :].astype(F32), (16, ATOMS_DEV))
        slots[SLOTS_HALF + s] = (lent_id - 256.0).astype(BF16)
        slots[2 * SLOTS_HALF + s] = (lent_id - 512.0).astype(BF16)

    one = jnp.ones((16, ATOMS_DEV), BF16)
    nil = jnp.zeros((16, ATOMS_DEV), BF16)

    def count_rows(first_slot, base, first_row, rows):
        @pl.loop(0, rows // 64)
        def _(tile):
            which = [
                (iota((16, ATOMS_DEV), 0) + (tile * 64 + base + 16 * r)).astype(F32).astype(BF16)
                for r in range(4)
            ]
            total = [nil] * 4
            for s in range(first_slot, first_slot + SLOTS_HALF):
                ids = slots[s]
                total = [t + jnp.where(ids == w, one, nil) for t, w in zip(total, which)]
            for r in range(4):
                place = pl.ds(pl.multiple_of(tile * 64 + (first_row + 16 * r), 16), 16)
                count[place, :] = total[r]

    count_rows(0, 0, 0, 256)
    count_rows(2 * SLOTS_HALF, 128, 256, 128)
    count_rows(SLOTS_HALF, 128 * (1 - odd_x), 384, 128)
    count_rows(SLOTS_HALF, 128 * odd_x, 512, 128)
    count_rows(2 * SLOTS_HALF, 0, 640, 128)

    centre = own[0:3]

    def radial_rows(target, begin, many):
        rows = 32
        for tile in range(many // rows):
            first = begin + tile * rows
            squared = None
            for c in range(3):
                gap = col[first : first + rows, c : c + 1] - pos_ref[c : c + 1, :]
                squared = gap * gap if squared is None else squared + gap * gap
            off = squared * (2.0 * ROOT_LOG2E) - 4.0 * ROOT_LOG2E
            grow = squared * (4.0 * LOG2E)
            up = jnp.exp2(grow - 9.0 * LOG2E)
            down = jnp.exp2(7.0 * LOG2E - grow)
            mid = jnp.exp2(-(off * off)) * count[first : first + rows, :].astype(F32)

            def put(k, value):
                target[k * many + tile * rows : k * many + (tile + 1) * rows, :] = value.astype(BF16)

            put(4, mid)
            value = mid
            for k in (5, 6, 7):
                value = value * up
                put(k, value)
                up = up * DROP
            value = mid
            for k in (3, 2, 1, 0):
                value = value * down
                put(k, value)
                down = down * DROP

    def left_rows(packed):
        n = packed.shape[1]
        eight = iota((8, n), 0).astype(F32)
        hot = jnp.where(packed[3:4] == eight, 1.0, 0.0)
        hot_high = jnp.where(packed[3:4] == eight - 4.0, 1.0, 0.0)
        p_high, p_low = split(packed[0:3])
        place = jnp.concatenate([p_high, p_low, jnp.zeros((2, n), F32)], axis=0)
        blank = jnp.zeros((8, n), F32)
        even = jnp.concatenate([hot, place, blank, blank], axis=0)
        odd = jnp.concatenate([hot_high, blank, place, blank], axis=0)
        return jnp.concatenate([even.astype(BF16), odd.astype(BF16)], axis=1), hot

    def gather_sums(both, target):
        wide = target.shape[0] // 4
        return [dot(both, target[q * wide : (q + 1) * wide, :]) for q in range(4)]

    col[0:256, :] = own.T
    radial_rows(rad_own, 0, 256)
    both_own, hot_own = left_rows(own)
    for q, s in enumerate(gather_sums(both_own, rad_own)):
        sent[q] = s

    filt = filt_ref[...].astype(F32)
    emb = emb_ref[...].astype(F32)
    emb8 = jnp.concatenate([emb, emb], axis=0)
    upper = iota((8, WIDTH), 0) < 4
    first_w = jnp.concatenate(
        [
            SCALE * emb8 * jnp.where(upper, filt[0, 2 * q : 2 * q + 1], filt[0, 2 * q + 1 : 2 * q + 2])
            for q in range(4)
        ],
        axis=0,
    )
    w_high, w_low = split(first_w)
    w_msg[...] = jnp.concatenate([w_high, w_high, w_low, jnp.where(upper, emb8, 0.0), SCALE * filt[1], jnp.zeros((16, WIDTH), F32)], axis=0).T.astype(BF16)
    for k in range(KB):
        ones = jnp.where(iota((128, 128), 0) == 104 + k, 1.0, 0.0).astype(BF16)
        fbc[k] = dot(w_msg[...], ones).astype(BF16)
    lane_low = iota((8, 128), 1) < 64
    sub = iota((8, 128), 0)

    def pair(first, axis):
        step = jnp.where(sub == axis, 1.0, 0.0)
        return jnp.where(lane_low, pack_recv[first] - step, pack_recv[first + 1] + step)

    near = jnp.where(sub == 0, step_x.astype(F32), 0.0)
    lent_hot = {}
    sums = [sent[q] for q in range(4)]
    for c in pack_copies[slice(2, 3)]:
        c.wait_recv()
    lent = pack_recv[2] + near
    col[384:512, :] = lent.T
    radial_rows(rad_pair, 384, 128)
    both_lent, lent_hot["p"] = left_rows(lent)
    sums = [a + b for a, b in zip(sums, gather_sums(both_lent, rad_pair))]

    for c in pack_copies[slice(0, 2)]:
        c.wait_recv()
    lent = pair(0, 2)
    col[256:384, :] = lent.T
    radial_rows(rad_z, 256, 128)
    both_lent, lent_hot["z"] = left_rows(lent)
    sums = [a + b for a, b in zip(sums, gather_sums(both_lent, rad_z))]

    for c in pack_copies[slice(3, 4)]:
        c.wait_recv()
    lent = pack_recv[3] - near
    col[512:640, :] = lent.T
    radial_rows(rad_x, 512, 128)
    both_lent, lent_hot["x"] = left_rows(lent)
    sums = [a + b for a, b in zip(sums, gather_sums(both_lent, rad_x))]

    for c in pack_copies[slice(4, 6)]:
        c.wait_recv()
    lent = pair(4, 1)
    col[640:768, :] = lent.T
    radial_rows(rad_y, 640, 128)
    both_lent, lent_hot["y"] = left_rows(lent)
    sums = [a + b for a, b in zip(sums, gather_sums(both_lent, rad_y))]

    agg = jnp.concatenate([s[0:8] for s in sums], axis=0)
    a_high, a_low = split(agg)
    chosen = dot(jnp.concatenate([a_high, a_low], axis=0).astype(BF16), sel[...])
    chosen = chosen[0:32] + chosen[32:64]
    for g in range(4):
        agg_send[g] = chosen[:, g * 128 : (g + 1) * 128]
    agg_copies = sends(agg_send, agg_recv, 6)
    for n in (3, 4, 5, 0, 1, 2):
        agg_copies[n].start()

    loads[5].wait()
    loads[6].wait()
    for l in range(2):
        for m in range(MODELS):
            uvt[l, m, :, 0:128] = u_vm[l, m].astype(F32).T.astype(BF16)
            uvt[l, m, :, 128:256] = v_vm[l, m].astype(F32).T.astype(BF16)

    for q in range(4):
        for odd in range(2):
            k = 2 * q + odd
            weight = jnp.sum(sums[q][4 * odd : 4 * odd + 4], axis=0, keepdims=True)
            base = 8 + 8 * odd
            for c in range(3):
                dsum[c, k : k + 1, :] = (
                    sums[q][base + c : base + c + 1]
                    + sums[q][base + 3 + c : base + 4 + c]
                    - centre[c : c + 1] * weight
                )

    def first_layer(table, hot):
        n = table.shape[1]
        t_high, t_low = split(table)
        blank = jnp.zeros((32, n), F32)
        x = jnp.concatenate([t_high, t_low, t_high, blank], axis=0).astype(BF16)
        z = jnp.concatenate([blank, blank, blank, hot, blank[0:24]], axis=0).astype(BF16)
        result = []
        for m in range(MODELS):
            rows = slice(m * C, (m + 1) * C)
            msg = dot(w_msg[rows, :], x).astype(BF16)
            h = dot(w_msg[rows, :], z)
            pre = dot(uvt[0, m], jnp.concatenate([msg, h.astype(BF16)], axis=0))
            result.append(add_silu(h, pre))
        return result

    def messages(m, h, part):
        rows = slice(m * C, (m + 1) * C)
        tiles = []
        for k in range(KB):
            for half in range(h.shape[1] // 128):
                tiles.append(h[:, half * 128 : (half + 1) * 128] * fbc[k, rows, :])
        return dot(jnp.concatenate(tiles, axis=1), part[...])

    for m, h in enumerate(first_layer(agg, hot_own)):
        rows = slice(m * C, (m + 1) * C)
        h_own[rows, :] = h
        acc[rows, :] = messages(m, h.astype(BF16), rad_own)

    wide_low = iota((32, 128), 1) < 64

    def agg_pair(first):
        return jnp.where(wide_low, agg_recv[first], agg_recv[first + 1])

    for c in agg_copies[slice(2, 3)]:
        c.wait_recv()
    for m, h in enumerate(first_layer(agg_recv[2], lent_hot["p"])):
        rows = slice(m * C, (m + 1) * C)
        acc[rows, :] += messages(m, h.astype(BF16), rad_pair)
    for c in agg_copies[slice(0, 2)]:
        c.wait_recv()
    for m, h in enumerate(first_layer(agg_pair(0), lent_hot["z"])):
        rows = slice(m * C, (m + 1) * C)
        acc[rows, :] += messages(m, h.astype(BF16), rad_z)
    for c in agg_copies[slice(3, 4)]:
        c.wait_recv()
    for m, h in enumerate(first_layer(agg_recv[3], lent_hot["x"])):
        rows = slice(m * C, (m + 1) * C)
        acc[rows, :] += messages(m, h.astype(BF16), rad_x)
    for c in agg_copies[slice(4, 6)]:
        c.wait_recv()
    message = []
    for m, h in enumerate(first_layer(agg_pair(4), lent_hot["y"])):
        rows = slice(m * C, (m + 1) * C)
        message.append((acc[rows, :] + messages(m, h.astype(BF16), rad_y)).astype(BF16))

    forces = []
    for m in range(MODELS):
        rows = slice(m * C, (m + 1) * C)
        x = jnp.concatenate([message[m], h_own[rows, :].astype(BF16)], axis=0)
        h = add_silu(h_own[rows, :], dot(uvt[1, m], x))
        coeff = dot(fw_ref[m], h.astype(BF16))
        forces.append([SCALE * jnp.sum(coeff * dsum[c], axis=0, keepdims=True) for c in range(3)])
    loads[7].wait()
    alive = jnp.where(iota((1, ATOMS_DEV), 1) < live_ref[0], 1.0, 0.0)
    spread = jnp.zeros((1, ATOMS_DEV), F32)
    for c in range(3):
        mean = (forces[0][c] + forces[1][c] + forces[2][c] + forces[3][c]) * 0.25
        for m in range(MODELS):
            gap = forces[m][c] - mean
            spread = spread + gap * gap
        mean_ref[c : c + 1, :] = mean * alive
    dev_ref[...] = spread * 0.25 * alive

    for c in pack_copies + agg_copies:
        c.wait_send()


def solution(mesh):
    sizes = tuple(mesh.shape[a] for a in AXES)

    def local(positions, species, neighbors, atom_count, ghost_x, ghost_yz, embedding, filters, update_u, update_v, force_w):
        vmem = pl.BlockSpec(memory_space=pltpu.VMEM)
        anywhere = pl.BlockSpec(memory_space=pl.ANY)
        mean, spread = pl.pallas_call(
            functools.partial(kernel, sizes),
            out_shape=(pltpu.VMEM((3, ATOMS_DEV), F32), pltpu.VMEM((1, ATOMS_DEV), F32)),
            in_specs=[anywhere] * 6 + [vmem, vmem, anywhere, anywhere, vmem],
            out_specs=(vmem, vmem),
            scratch_shapes=[
                pltpu.VMEM((3, ATOMS_DEV), F32),
                pltpu.VMEM((1, ATOMS_DEV), jnp.int32),
                pltpu.VMEM((2 * SLOTS_HALF, ATOMS_DEV), jnp.int32),
                pltpu.SMEM((1,), jnp.int32),
                pltpu.VMEM((2, 128), jnp.int32),
                pltpu.VMEM((4, 64), jnp.int32),
                pltpu.VMEM((2, MODELS, C, C), BF16),
                pltpu.VMEM((2, MODELS, C, C), BF16),
                pltpu.VMEM((ATOMS_DEV, GHOSTS), BF16),
                pltpu.VMEM((4, 8, 128), F32),
                pltpu.VMEM((6, 8, 128), F32),
                pltpu.VMEM((4, 32, 128), F32),
                pltpu.VMEM((6, 32, 128), F32),
                pltpu.VMEM((3 * SLOTS_HALF, 16, ATOMS_DEV), BF16),
                pltpu.VMEM((TABLE, ATOMS_DEV), BF16),
                pltpu.VMEM((TABLE, 8), F32),
                pltpu.VMEM((KB * 256, ATOMS_DEV), BF16),
                pltpu.VMEM((KB * 128, ATOMS_DEV), BF16),
                pltpu.VMEM((KB * 128, ATOMS_DEV), BF16),
                pltpu.VMEM((KB * 128, ATOMS_DEV), BF16),
                pltpu.VMEM((KB * 128, ATOMS_DEV), BF16),
                pltpu.VMEM((WIDTH, ATOMS_DEV), F32),
                pltpu.VMEM((WIDTH, KB * 256), BF16),
                pltpu.VMEM((WIDTH, ATOMS_DEV), F32),
                pltpu.VMEM((KB, WIDTH, 128), BF16),
                pltpu.VMEM((2, MODELS, C, 2 * C), BF16),
                pltpu.VMEM((WIDTH, 128), BF16),
                pltpu.VMEM((3, KB, ATOMS_DEV), F32),
                pltpu.VMEM((4, 32, ATOMS_DEV), F32),
                pltpu.SemaphoreType.DMA((12,)),
                pltpu.SemaphoreType.DMA((12,)),
                pltpu.SemaphoreType.DMA((8,)),
            ],
            compiler_params=pltpu.CompilerParams(
                collective_id=0, has_side_effects=True, vmem_limit_bytes=60 * 1024 * 1024
            ),
        )(
            positions,
            species.reshape(1, ATOMS_DEV),
            neighbors,
            atom_count,
            ghost_x.reshape(2, 2 * 64),
            ghost_yz.reshape(4, 64),
            embedding,
            filters,
            update_u,
            update_v,
            jnp.swapaxes(force_w, 1, 2),
        )
        return mean, spread.reshape(ATOMS_DEV)

    split_spec = P(AXES)
    return jax.shard_map(
        local,
        mesh=mesh,
        in_specs=(
            P(None, AXES), split_spec, P(None, AXES), split_spec,
            P(AXES, None, None), P(AXES, None, None), P(), P(), P(), P(), P(),
        ),
        out_specs=(P(None, AXES), split_spec),
        check_vma=False,
    )
```
